256 devices in a mesh: group: 32 (over x, z_hi, core), head: 8 (over z_lo, y).
Axes of the slice: x: 4, y: 4, z: 8 (z_hi: 4, z_lo: 2; z = z_hi * 2 + z_lo), core: 2. Of those that a mesh axis runs over, the one named last changes fastest.
Arguments:
- query: bfloat16 [32, 512, 5120], P('group', None, 'head'), may hold values from -1.7265625 to 1.7265625
- key: bfloat16 [32, 512, 5120], P('group', None, 'head'), may hold values from -1.7265625 to 1.7265625
- value: bfloat16 [32, 512, 5120], P('group', None, 'head'), may hold values from -6 to 6
- output: bfloat16 [32, 512, 5120], P('group', None, 'head'), may hold values from -1.5 to 1.5
- grad_out: bfloat16 [32, 512, 5120], P('group', 'head'), may hold values from -169 to 169
- log_sum: float32 [32, 40, 512], P('group', 'head'), as said below
- group_length: int32 [32], replicated, may hold values from 256 to 512, as said below
- cache_source: int32 [32], replicated, may hold values from -1 to 30, as said below
Outputs:
- grad_query: bfloat16 [32, 512, 5120], P('group', 'head')
- grad_key: bfloat16 [32, 512, 5120], P('group', 'head')
- grad_value: bfloat16 [32, 512, 5120], P('group', 'head')
The draws below stay inside these ranges and needn't reach their ends.
Inputs may be any that keep to these rules, and one draw needn't show every extreme that they name: group_length[c] counts the first, live token slots of group c; some group is full. cache_source[c] is c - 1 where group c attends the preceding group's cache and -1 where a rollout starts; it is -1 for group 0 and c - 1 for the last group. `log_sum`: each entry lies between ln(512) + 0.2 and ln(1024) + 0.8.
All inputs are finite; a program needn't handle non-finite values.
Results may differ from the reference program's by a relative error of at most 0.0049.
Values may be sent and summed in bfloat16 or wider, within the bound.
A program may use at most 128 MiB of HBM per device.

```python
import math
import jax
import jax.numpy as jnp
from jax import lax

HEADS = 40
HEAD_DIM = 128
LEN = 512
GROUPS = 32


def draw_group_length(key, part):
    lengths = jax.random.randint(jax.random.fold_in(key, 11), (GROUPS,), LEN // 2, LEN + 1)
    full_at = jax.random.randint(jax.random.fold_in(key, 12), (), 0, GROUPS)
    return jnp.where(jnp.arange(GROUPS) == full_at, LEN, lengths).astype(jnp.int32)


def draw_cache_source(key, part):
    group_ids = jnp.arange(GROUPS, dtype=jnp.int32)
    linked = jax.random.randint(jax.random.fold_in(key, 21), (GROUPS,), 0, 4) > 0
    linked = linked & (group_ids > 0) | (group_ids == GROUPS - 1)
    return jnp.where(linked, group_ids - 1, -1).astype(jnp.int32)


def draw_log_sum(key, part):
    lower = math.log(LEN) + 0.2
    upper = math.log(2 * LEN) + 0.8
    unit = jax.random.uniform(jax.random.fold_in(key, 31), (GROUPS, HEADS, LEN), jnp.float32)
    return (lower + (upper - lower) * unit).astype(jnp.float32)


def block_levels(stream_key, dims, cuts, least, high):
    def one(axis_at, shards_of):
        steps = jax.random.uniform(jax.random.fold_in(jax.random.fold_in(stream_key, 6), axis_at), (shards_of,), jnp.float32, least / len(cuts), high / len(cuts))
        return jnp.repeat(jnp.exp(steps), dims[axis_at] // shards_of).reshape((-1,) + (1,) * (len(dims) - axis_at - 1))

    gain = one(*cuts[0])
    for cut in cuts[1:]:
        gain = gain * one(*cut)
    return gain


def centred(stream_key, dims, width, bound, shards=(), kind=jnp.bfloat16):
    gain = block_levels(stream_key, dims, shards, -0.22, 0.18) if shards else 1.0
    result = jax.random.normal(stream_key, dims, jnp.float32) * width * gain
    return jnp.minimum(jnp.maximum(result, -bound), bound).astype(kind)


def setup_inputs(seed: int = 0) -> dict:
    streams_of = jax.random.split(jax.random.key(seed), 9)
    return {
        "query": jnp.clip(jax.random.uniform(streams_of[0], (GROUPS, LEN, HEADS * HEAD_DIM), jnp.float32, -1.7265625, 1.7265625) * block_levels(streams_of[0], (GROUPS, LEN, HEADS * HEAD_DIM), ((0, 32), (2, 8)), -0.4, 0.0), -1.7265625, 1.7265625).astype(jnp.bfloat16),
        "key": jnp.clip(jax.random.uniform(streams_of[1], (GROUPS, LEN, HEADS * HEAD_DIM), jnp.float32, -1.7265625, 1.7265625) * block_levels(streams_of[1], (GROUPS, LEN, HEADS * HEAD_DIM), ((0, 32), (2, 8)), -0.4, 0.0), -1.7265625, 1.7265625).astype(jnp.bfloat16),
        "value": centred(streams_of[2], (GROUPS, LEN, HEADS * HEAD_DIM), 1.0, 6.0, ((0, 32), (2, 8))),
        "output": centred(streams_of[3], (GROUPS, LEN, HEADS * HEAD_DIM), 0.25, 1.5, ((0, 32), (2, 8))),
        "grad_out": centred(streams_of[4], (GROUPS, LEN, HEADS * HEAD_DIM), (1.25 * LEN ** 0.5), 169.0, ((0, 32), (1, 8))),
        "log_sum": draw_log_sum(jax.random.fold_in(streams_of[8], 71), 0),
        "group_length": draw_group_length(jax.random.fold_in(streams_of[8], 71), 0),
        "cache_source": draw_cache_source(jax.random.fold_in(streams_of[8], 71), 0),
    }


def tile_grads(query_rows, grad_rows, lse_row, delta_row, key_rows, value_rows, alive_mask):
    score_scale = query_rows.shape[-1] ** -0.5
    scores = jnp.dot(query_rows, key_rows.T, preferred_element_type=jnp.float32) * score_scale
    attn_prob = jnp.where(alive_mask, jnp.exp(scores - lse_row[:, None]), 0.0)
    prob_half = attn_prob.astype(jnp.bfloat16)
    grad_prob = jnp.dot(grad_rows, value_rows.T, preferred_element_type=jnp.float32)
    grad_score = (attn_prob * (grad_prob - delta_row[:, None])).astype(jnp.bfloat16)
    grad_v = jnp.dot(prob_half.T, grad_rows, preferred_element_type=jnp.float32)
    grad_k = jnp.dot(grad_score.T, query_rows, preferred_element_type=jnp.float32) * score_scale
    grad_q = jnp.dot(grad_score, key_rows, preferred_element_type=jnp.float32) * score_scale
    return grad_q, grad_k, grad_v


def head_major(block):
    return block.reshape(LEN, HEADS, HEAD_DIM).transpose(1, 0, 2)


def token_major(block):
    return block.transpose(1, 0, 2).reshape(LEN, HEADS * HEAD_DIM)


def reference(query, key, value, output, grad_out, log_sum, group_length, cache_source):
    group_ids = jnp.arange(GROUPS, dtype=jnp.int32)
    linked = cache_source == group_ids - 1
    prev_length = jnp.concatenate([jnp.zeros((1,), jnp.int32), group_length[:-1]])
    prev_key = jnp.concatenate([jnp.zeros_like(key[:1]), key[:-1]], axis=0)
    prev_value = jnp.concatenate([jnp.zeros_like(value[:1]), value[:-1]], axis=0)
    row_index = jnp.arange(LEN, dtype=jnp.int32)

    def step(carry, inputs):
        carry_k, carry_v = carry
        q_c, k_c, v_c, o_c, g_c, lse_c, pk_c, pv_c, own_len, prev_len, link_c = inputs
        row_delta = jnp.sum((g_c.astype(jnp.float32) * o_c.astype(jnp.float32)).reshape(LEN, HEADS, HEAD_DIM), axis=2).T
        own_rows = row_index < own_len
        self_mask = own_rows[:, None] & own_rows[None, :]
        cross_mask = own_rows[:, None] & ((row_index < prev_len) & link_c)[None, :]

        def per_head(items):
            qh, gh, lh, dh, kh, vh, pkh, pvh = items
            sq, sk, sv = tile_grads(qh, gh, lh, dh, kh, vh, self_mask)
            xq, xk, xv = tile_grads(qh, gh, lh, dh, pkh, pvh, cross_mask)
            return sq + xq, sk, sv, xk, xv

        hq, hk, hv, hxk, hxv = lax.map(per_head, (head_major(q_c), head_major(g_c), lse_c, row_delta, head_major(k_c), head_major(v_c), head_major(pk_c), head_major(pv_c)))
        out_q = token_major(hq).astype(jnp.bfloat16)
        out_k = (token_major(hk) + carry_k).astype(jnp.bfloat16)
        out_v = (token_major(hv) + carry_v).astype(jnp.bfloat16)
        return (token_major(hxk), token_major(hxv)), (out_q, out_k, out_v)

    start = (jnp.zeros((LEN, HEADS * HEAD_DIM), jnp.float32), jnp.zeros((LEN, HEADS * HEAD_DIM), jnp.float32))
    _, outs = lax.scan(step, start, (query, key, value, output, grad_out, log_sum, prev_key, prev_value, group_length, prev_length, linked), reverse=True)
    return outs[0], outs[1], outs[2]
```

```python
import functools
import math

import jax
import jax.numpy as jnp
from jax import lax
from jax.experimental import pallas as pl
from jax.experimental.pallas import tpu as pltpu
from jax.sharding import PartitionSpec as P

HEAD_DIM = 128
MESH = pl.DeviceIdType.MESH
SCALE = HEAD_DIM**-0.5
LOG2E = math.log2(math.e)
DEAD = 1e30


def dot_nt(a, b):
    return lax.dot_general(a, b, (((1,), (1,)), ((), ())), preferred_element_type=jnp.float32)


def dot_nn(a, b):
    return jnp.dot(a, b, preferred_element_type=jnp.float32)


def block_grads(q, g, lse_row, delta_row, k, kt, v):
    prob = jnp.exp2(dot_nt(k, q) * (SCALE * LOG2E) - lse_row)
    grad_score = (prob * (dot_nt(v, g) - delta_row)).astype(jnp.bfloat16)
    grad_v = dot_nn(prob.astype(jnp.bfloat16), g)
    grad_k = dot_nn(grad_score, q)
    grad_q = dot_nn(kt, grad_score).T
    return grad_q, grad_k, grad_v


def kernel(
    len_ref, source_ref, q_hbm, k_hbm, v_hbm, o_hbm, g_hbm, lse_ref,
    out_q, out_k, out_v,
    q_own, k_own, v_own, o_own, g_own, q_next, g_next, lse_next, delta_own, delta_next,
    acc_q, acc_k, acc_v, stage, cross_q, cross_in,
    load_sem, local_sem, g_send, g_recv, lse_sem, q_sem, fwd_sem, delta_sem, cross_sem,
    out_send, out_recv, out_local,
):
    heads, length, _ = q_own.shape
    groups = lax.axis_size("group")
    parts = lax.axis_size("head")
    rows = length // parts
    group, me = lax.axis_index("group"), lax.axis_index("head")
    after, before = lax.rem(group + 1, groups), lax.rem(group + groups - 1, groups)

    def lanes(i):
        return pl.ds(pl.multiple_of(i * HEAD_DIM, HEAD_DIM), HEAD_DIM)

    def token_rows(part):
        return pl.ds(pl.multiple_of(part * rows, rows), rows)

    def to(src, dst, sems, slot, device):
        return pltpu.make_async_remote_copy(
            src_ref=src, dst_ref=dst, send_sem=sems.at[0, slot], recv_sem=sems.at[1, slot],
            device_id=device, device_id_type=MESH,
        )

    def loads(i):
        pairs = ((k_hbm, k_own), (v_hbm, v_own), (q_hbm, q_own), (o_hbm, o_own))
        return [
            pltpu.make_async_copy(src.at[0, :, lanes(i)], dst.at[i], load_sem.at[at, i])
            for at, (src, dst) in enumerate(pairs)
        ]

    def local_g(i):
        return pltpu.make_async_copy(
            g_hbm.at[0, :, lanes(me * heads + i)], g_own.at[i, token_rows(me)], local_sem.at[i]
        )

    def q_copy(i):
        return to(q_hbm.at[0, :, lanes(i)], q_next.at[i], q_sem, i, (before, me))

    def g_copy(i):
        return to(g_own.at[i], g_next.at[i], fwd_sem, i, (before, me))

    def delta_copy(i):
        return to(delta_own.at[i], delta_next.at[i], delta_sem, i, (before, me))

    def cross_copy(i):
        return to(cross_q.at[i], cross_in.at[i], cross_sem, i, (after, me))

    lse_copy = to(lse_ref.at[0], lse_next, lse_sem, 0, (before, me))

    barrier = pltpu.get_barrier_semaphore()

    @pl.loop(1, parts)
    def _(step):
        pl.semaphore_signal(
            barrier, inc=1, device_id=(group, lax.rem(me + step, parts)), device_id_type=MESH
        )

    for neighbour in (before, after):
        pl.semaphore_signal(barrier, inc=1, device_id=(neighbour, me), device_id_type=MESH)

    @pl.loop(0, heads)
    def _(i):
        local_g(i).start()
        for copy in loads(i):
            copy.start()

    pl.semaphore_wait(barrier, parts + 1)

    @pl.loop(0, heads)
    def _(i):
        @pl.loop(1, parts)
        def _(step):
            peer = lax.rem(me + step, parts)
            pltpu.make_async_remote_copy(
                src_ref=g_hbm.at[0, :, lanes(peer * heads + i)],
                dst_ref=g_own.at[i, token_rows(me)],
                send_sem=g_send, recv_sem=g_recv.at[i],
                device_id=(group, peer), device_id_type=MESH,
            ).start()

        q_copy(i).start()

    lse_copy.start()

    own_len = len_ref[group]
    after_len = jnp.where(source_ref[after] == group, len_ref[after], 0)
    query_at = lax.broadcasted_iota(jnp.int32, (1, length), 1)
    key_live = lax.broadcasted_iota(jnp.int32, (length, HEAD_DIM), 0) < own_len
    zero = jnp.zeros((), jnp.bfloat16)

    @pl.loop(0, heads)
    def _(i):
        others = g_own.at[i, pl.ds(0, (parts - 1) * rows)]
        pltpu.make_async_copy(others, others, g_recv.at[i]).wait()
        local_g(i).wait()
        g_copy(i).start()
        for copy in loads(i):
            copy.wait()
        g = g_own[i]
        product = g.astype(jnp.float32) * o_own[i].astype(jnp.float32)
        delta = jnp.sum(product.T, axis=0, keepdims=True)
        delta_own[i] = delta
        delta_copy(i).start()
        lse_row = jnp.where(query_at < own_len, lse_ref[0, pl.ds(i, 1), :] * LOG2E, DEAD)
        k = jnp.where(key_live, k_own[i], zero)
        grad_q, grad_k, grad_v = block_grads(q_own[i], g, lse_row, delta, k, k.T, v_own[i])
        acc_q[i] = grad_q
        acc_k[i] = grad_k
        acc_v[i] = grad_v

    lse_copy.wait_recv()

    def send_out(which, out, i):
        columns = lanes(me * heads + i)

        @pl.loop(1, parts)
        def _(step):
            peer = lax.rem(me + step, parts)
            pltpu.make_async_remote_copy(
                src_ref=stage.at[which, i, token_rows(peer)],
                dst_ref=out.at[0, :, columns],
                send_sem=out_send.at[which], recv_sem=out_recv.at[which],
                device_id=(group, peer), device_id_type=MESH,
            ).start()

        pltpu.make_async_copy(
            stage.at[which, i, token_rows(me)], out.at[0, :, columns], out_local.at[which]
        ).start()

    def finish_query(i):
        cross_copy(i).wait_recv()
        total = (acc_q[i] + cross_in[i].astype(jnp.float32)) * SCALE
        stage[0, i] = total.astype(jnp.bfloat16)
        send_out(0, out_q, i)

    @pl.loop(0, heads)
    def _(i):
        q_copy(i).wait_recv()
        g_copy(i).wait_recv()
        delta_copy(i).wait_recv()
        lse_row = jnp.where(query_at < after_len, lse_next[pl.ds(i, 1), :] * LOG2E, DEAD)
        k = jnp.where(key_live, k_own[i], zero)
        grad_q, grad_k, grad_v = block_grads(
            q_next[i], g_next[i], lse_row, delta_next[i], k, k.T, v_own[i]
        )
        cross_q[i] = grad_q.astype(jnp.bfloat16)
        cross_copy(i).start()
        sum_k = jnp.where(key_live, (acc_k[i] + grad_k) * SCALE, 0.0)
        stage[1, i] = sum_k.astype(jnp.bfloat16)
        send_out(1, out_k, i)
        sum_v = jnp.where(key_live, acc_v[i] + grad_v, 0.0)
        stage[2, i] = sum_v.astype(jnp.bfloat16)
        send_out(2, out_v, i)

        @pl.when(i > 0)
        def _():
            finish_query(i - 1)

    finish_query(heads - 1)

    for which, out in enumerate((out_q, out_k, out_v)):
        theirs = out.at[0, :, pl.ds(0, (parts - 1) * heads * HEAD_DIM)]
        mine = out.at[0, :, pl.ds(0, heads * HEAD_DIM)]
        pltpu.make_async_copy(theirs, theirs, out_recv.at[which]).wait()
        pltpu.make_async_copy(theirs, theirs, out_send.at[which]).wait()
        pltpu.make_async_copy(mine, mine, out_local.at[which]).wait()
    sent = g_hbm.at[0, :, pl.ds(0, (parts - 1) * heads * HEAD_DIM)]
    pltpu.make_async_copy(sent, sent, g_send).wait()
    lse_copy.wait_send()

    @pl.loop(0, heads)
    def _(i):
        q_copy(i).wait_send()
        g_copy(i).wait_send()
        delta_copy(i).wait_send()
        cross_copy(i).wait_send()


def on_device(query, key, value, output, grad_out, log_sum, group_length, cache_source):
    _, length, features = query.shape
    heads = features // HEAD_DIM
    per_head = (heads, length, HEAD_DIM)
    half = pltpu.VMEM(per_head, jnp.bfloat16)
    wide = pltpu.VMEM(per_head, jnp.float32)
    row = pltpu.VMEM((heads, 1, length), jnp.float32)
    dma = pltpu.SemaphoreType.DMA
    anywhere = pl.BlockSpec(memory_space=pl.ANY)
    smem = pl.BlockSpec(memory_space=pltpu.SMEM)
    out = jax.ShapeDtypeStruct(grad_out.shape, jnp.bfloat16)
    flops = 10 * 2 * heads * length * length * HEAD_DIM
    return pl.pallas_call(
        kernel,
        out_shape=(out, out, out),
        in_specs=[smem, smem] + [anywhere] * 5 + [pl.BlockSpec(memory_space=pltpu.VMEM)],
        out_specs=(anywhere, anywhere, anywhere),
        scratch_shapes=[
            half, half, half, half, half, half, half,
            pltpu.VMEM((heads, length), jnp.float32), row, row,
            wide, wide, wide,
            pltpu.VMEM((3,) + per_head, jnp.bfloat16), half, half,
            dma((4, heads)), dma((heads,)), dma, dma((heads,)), dma((2, 1)), dma((2, heads)),
            dma((2, heads)), dma((2, heads)), dma((2, heads)),
            dma((3,)), dma((3,)), dma((3,)),
        ],
        compiler_params=pltpu.CompilerParams(
            collective_id=0, has_side_effects=True, vmem_limit_bytes=48 * 1024 * 1024
        ),
        cost_estimate=pl.CostEstimate(
            flops=flops, bytes_accessed=8 * length * features * 2, transcendentals=2 * heads * length * length
        ),
        name="attention_backward",
    )(group_length, cache_source, query, key, value, output, grad_out, log_sum)


def solution(mesh):
    by_head, by_token = P("group", None, "head"), P("group", "head", None)
    return jax.shard_map(
        on_device,
        mesh=mesh,
        in_specs=(by_head, by_head, by_head, by_head, by_token, by_token, P(), P()),
        out_specs=(by_token, by_token, by_token),
        check_vma=False,
    )
```

```python
import functools
import math

import jax
import jax.numpy as jnp
from jax import lax
from jax.experimental import pallas as pl
from jax.experimental.pallas import tpu as pltpu
from jax.sharding import PartitionSpec as P

HEAD_DIM = 128
MESH = pl.DeviceIdType.MESH
SCALE = HEAD_DIM**-0.5
LOG2E = math.log2(math.e)
DEAD = 1e30


def dot_nt(a, b):
    return lax.dot_general(a, b, (((1,), (1,)), ((), ())), preferred_element_type=jnp.float32)


def dot_nn(a, b):
    return jnp.dot(a, b, preferred_element_type=jnp.float32)


def block_grads(q, g, lse_row, delta_row, k, kt, v):
    prob = jnp.exp2(dot_nt(k, q) * (SCALE * LOG2E) - lse_row)
    grad_score = (prob * (dot_nt(v, g) - delta_row)).astype(jnp.bfloat16)
    grad_v = dot_nn(prob.astype(jnp.bfloat16), g)
    grad_k = dot_nn(grad_score, q)
    grad_q = dot_nn(kt, grad_score).T
    return grad_q, grad_k, grad_v


def kernel(
    len_ref, source_ref, q_hbm, k_hbm, v_hbm, o_hbm, g_hbm, lse_ref,
    out_q, out_k, out_v,
    q_own, k_own, v_own, o_own, g_own, moved_a, moved_b, lse_next, delta_own, delta_next,
    acc_q, acc_k, acc_v, stage, cross_out, cross_in, land, land_far,
    load_sem, local_sem, g_send, g_recv, lse_sem, a_sem, b_sem, low_sem, direct_send, delta_sem,
    near_sem, far_send, far_recv, out_send, out_recv, out_local,
):
    heads, length, _ = q_own.shape
    groups = lax.axis_size("group")
    parts = lax.axis_size("head")
    half = parts // 2
    rows = length // parts
    group, me = lax.axis_index("group"), lax.axis_index("head")
    after, before = lax.rem(group + 1, groups), lax.rem(group + groups - 1, groups)
    even = lax.rem(group, 2) == 0
    odd = lax.rem(group, 2) == 1
    lower = me < half
    upper = me >= half
    near = lax.rem(group, 2) * before + (1 - lax.rem(group, 2)) * after
    far = lax.rem(group, 2) * after + (1 - lax.rem(group, 2)) * before

    def lanes(i):
        return pl.ds(pl.multiple_of(i * HEAD_DIM, HEAD_DIM), HEAD_DIM)

    def token_rows(part):
        return pl.ds(pl.multiple_of(part * rows, rows), rows)

    low_rows, high_rows = pl.ds(0, length // 2), pl.ds(length // 2, length // 2)

    def to(src, dst, send, recv, device):
        return pltpu.make_async_remote_copy(
            src_ref=src, dst_ref=dst, send_sem=send, recv_sem=recv,
            device_id=device, device_id_type=MESH,
        )

    def wait_bytes(ref, sem):
        pltpu.make_async_copy(ref, ref, sem).wait()

    def loads(i):
        pairs = ((k_hbm, k_own), (v_hbm, v_own), (q_hbm, q_own), (o_hbm, o_own))
        return [
            pltpu.make_async_copy(src.at[0, :, lanes(i)], dst.at[i], load_sem.at[at, i])
            for at, (src, dst) in enumerate(pairs)
        ]

    def local_g(i):
        return pltpu.make_async_copy(
            g_hbm.at[0, :, lanes(me * heads + i)], g_own.at[i, token_rows(me)], local_sem.at[i]
        )

    def key_copy(i):
        return to(k_hbm.at[0, :, lanes(i)], moved_a.at[i], a_sem.at[0, i], a_sem.at[1, i], (after, me))

    def value_copy(i):
        return to(v_hbm.at[0, :, lanes(i)], moved_b.at[i], b_sem.at[0, i], b_sem.at[1, i], (after, me))

    def query_copy(i):
        return to(q_hbm.at[0, :, lanes(i)], moved_a.at[i], a_sem.at[0, i], a_sem.at[1, i], (before, me))

    def g_high_copy(i):
        return to(
            g_own.at[i, high_rows], moved_b.at[i, high_rows], b_sem.at[0, i], b_sem.at[1, i], (before, me)
        )

    def g_low_copy(i):
        return to(
            g_own.at[i, low_rows], moved_b.at[i, low_rows], low_sem.at[0, i], low_sem.at[1, i], (before, me)
        )

    def delta_copy(i):
        return to(delta_own.at[i], delta_next.at[i], delta_sem.at[0, i], delta_sem.at[1, i], (before, me))

    def near_copy(which, i):
        return to(
            cross_out.at[which, i], cross_in.at[which, i],
            near_sem.at[0, which, i], near_sem.at[1, which, i], (near, me),
        )

    lse_copy = to(lse_ref.at[0], lse_next, lse_sem.at[0], lse_sem.at[1], (before, me))

    barrier = pltpu.get_barrier_semaphore()

    @pl.loop(1, parts)
    def _(step):
        pl.semaphore_signal(
            barrier, inc=1, device_id=(group, lax.rem(me + step, parts)), device_id_type=MESH
        )

    @pl.loop(0, parts)
    def _(part):
        pl.semaphore_signal(barrier, inc=1, device_id=(far, part), device_id_type=MESH)

    pl.semaphore_signal(barrier, inc=1, device_id=(near, me), device_id_type=MESH)

    @pl.loop(0, heads)
    def _(i):
        local_g(i).start()
        for copy in loads(i):
            copy.start()

    pl.semaphore_wait(barrier, 2 * parts)

    @pl.loop(0, heads)
    def _(i):
        @pl.loop(1, parts)
        def _(step):
            peer = lax.rem(me + step, parts)
            to(
                g_hbm.at[0, :, lanes(peer * heads + i)], g_own.at[i, token_rows(me)],
                g_send, g_recv.at[i], (group, peer),
            ).start()

        @pl.when(even & lower)
        def _():
            @pl.loop(0, half)
            def _(step):
                peer = half + lax.rem(me + step, half)
                to(
                    g_hbm.at[0, :, lanes(peer * heads + i)], moved_b.at[i, token_rows(me)],
                    direct_send, low_sem.at[1, i], (before, peer),
                ).start()

        @pl.when(lower)
        def _():
            key_copy(i).start()
            value_copy(i).start()

        @pl.when(upper)
        def _():
            query_copy(i).start()

    own_len, before_len = len_ref[group], len_ref[before]
    linked_len = jnp.where(source_ref[group] == before, own_len, 0)
    after_len = jnp.where(source_ref[after] == group, len_ref[after], 0)
    query_at = lax.broadcasted_iota(jnp.int32, (1, length), 1)
    key_at = lax.broadcasted_iota(jnp.int32, (length, HEAD_DIM), 0)
    zero = jnp.zeros((), jnp.bfloat16)

    def own_row(i, live):
        return jnp.where(query_at < live, lse_ref[0, pl.ds(i, 1), :] * LOG2E, DEAD)

    def live_keys(k, live):
        return jnp.where(key_at < live, k, zero)

    def half_rows(x, live):
        return jnp.where(key_at < live, x, 0.0).astype(jnp.bfloat16)

    def send_out(which, i):
        columns = lanes(me * heads + i)

        @pl.loop(1, parts)
        def _(step):
            peer = lax.rem(me + step, parts)
            to(
                stage.at[which, i, token_rows(peer)], land.at[which, :, columns],
                out_send.at[which], out_recv.at[which], (group, peer),
            ).start()

        pltpu.make_async_copy(
            stage.at[which, i, token_rows(me)], land.at[which, :, columns], out_local.at[which]
        ).start()

    def send_far(which, i):
        columns = lanes(lax.rem(me, half) * heads + i)

        @pl.loop(0, parts)
        def _(step):
            peer = lax.rem(me + step, parts)
            to(
                cross_out.at[which, i, token_rows(peer)], land_far.at[which, :, columns],
                far_send.at[which], far_recv.at[which], (far, peer),
            ).start()

    def wait_g(i):
        wait_bytes(g_own.at[i, pl.ds(0, (parts - 1) * rows)], g_recv.at[i])
        local_g(i).wait()

    def own_delta(i):
        product = g_own[i].astype(jnp.float32) * o_own[i].astype(jnp.float32)
        delta = jnp.sum(product.T, axis=0, keepdims=True)
        delta_own[i] = delta
        return delta

    def own_block(i, delta):
        k = live_keys(k_own[i], own_len)
        return block_grads(q_own[i], g_own[i], own_row(i, own_len), delta, k, k.T, v_own[i])

    @pl.when(lower)
    def _():
        def finish_keys(i):
            near_copy(0, i).wait_recv()
            stage[1, i] = (acc_k[i] + cross_in[0, i].astype(jnp.float32)).astype(jnp.bfloat16)
            send_out(1, i)
            near_copy(1, i).wait_recv()
            stage[2, i] = (acc_v[i] + cross_in[1, i].astype(jnp.float32)).astype(jnp.bfloat16)
            send_out(2, i)

        @pl.loop(0, heads)
        def _(i):
            wait_g(i)
            for copy in loads(i):
                copy.wait()
            grad_q, grad_k, grad_v = own_block(i, own_delta(i))
            acc_q[i] = grad_q
            grad_k = jnp.where(key_at < own_len, grad_k * SCALE, 0.0)
            grad_v = jnp.where(key_at < own_len, grad_v, 0.0)

            @pl.when(even)
            def _():
                acc_k[i] = grad_k
                acc_v[i] = grad_v

            @pl.when(odd)
            def _():
                stage[1, i] = grad_k.astype(jnp.bfloat16)
                send_out(1, i)
                stage[2, i] = grad_v.astype(jnp.bfloat16)
                send_out(2, i)

        @pl.loop(0, heads)
        def _(i):
            key_copy(i).wait_recv()
            value_copy(i).wait_recv()
            k = live_keys(moved_a[i], before_len)
            grad_q, grad_k, grad_v = block_grads(
                q_own[i], g_own[i], own_row(i, linked_len), delta_own[i], k, k.T, moved_b[i]
            )
            cross_out[0, i] = half_rows(grad_k * SCALE, before_len)
            cross_out[1, i] = half_rows(grad_v, before_len)

            @pl.when(odd)
            def _():
                near_copy(0, i).start()
                near_copy(1, i).start()

            @pl.when(even)
            def _():
                send_far(0, i)
                send_far(1, i)

            stage[0, i] = ((acc_q[i] + grad_q) * SCALE).astype(jnp.bfloat16)
            send_out(0, i)

            @pl.when(even & (i > 0))
            def _():
                finish_keys(i - 1)

        @pl.when(even)
        def _():
            finish_keys(heads - 1)
            wait_bytes(cross_out.at[0], far_send.at[0])
            wait_bytes(cross_out.at[1], far_send.at[1])
            wait_bytes(g_hbm.at[0, :, pl.ds(0, half * heads * HEAD_DIM)], direct_send)

        @pl.loop(0, heads)
        def _(i):
            key_copy(i).wait_send()
            value_copy(i).wait_send()

            @pl.when(odd)
            def _():
                near_copy(0, i).wait_send()
                near_copy(1, i).wait_send()

    @pl.when(upper)
    def _():
        lse_copy.start()

        def finish_query(i):
            near_copy(0, i).wait_recv()
            stage[0, i] = (acc_q[i] * SCALE + cross_in[0, i].astype(jnp.float32)).astype(jnp.bfloat16)
            send_out(0, i)

        @pl.loop(0, heads)
        def _(i):
            wait_g(i)
            g_high_copy(i).start()

            @pl.when(odd)
            def _():
                g_low_copy(i).start()

            for copy in loads(i):
                copy.wait()
            delta = own_delta(i)
            delta_copy(i).start()
            grad_q, grad_k, grad_v = own_block(i, delta)
            acc_k[i] = grad_k
            acc_v[i] = grad_v

            @pl.when(even)
            def _():
                stage[0, i] = (grad_q * SCALE).astype(jnp.bfloat16)
                send_out(0, i)

            @pl.when(odd)
            def _():
                acc_q[i] = grad_q

        lse_copy.wait_recv()

        @pl.loop(0, heads)
        def _(i):
            query_copy(i).wait_recv()
            g_high_copy(i).wait_recv()
            g_low_copy(i).wait_recv()
            delta_copy(i).wait_recv()
            lse_row = jnp.where(query_at < after_len, lse_next[pl.ds(i, 1), :] * LOG2E, DEAD)
            k = live_keys(k_own[i], own_len)
            grad_q, grad_k, grad_v = block_grads(
                moved_a[i], moved_b[i], lse_row, delta_next[i], k, k.T, v_own[i]
            )
            cross_out[0, i] = (grad_q * SCALE).astype(jnp.bfloat16)

            @pl.when(even)
            def _():
                near_copy(0, i).start()

            @pl.when(odd)
            def _():
                send_far(0, i)

            stage[1, i] = half_rows((acc_k[i] + grad_k) * SCALE, own_len)
            send_out(1, i)
            stage[2, i] = half_rows(acc_v[i] + grad_v, own_len)
            send_out(2, i)

            @pl.when(odd & (i > 0))
            def _():
                finish_query(i - 1)

        @pl.when(odd)
        def _():
            finish_query(heads - 1)
            wait_bytes(cross_out.at[0], far_send.at[0])

        lse_copy.wait_send()

        @pl.loop(0, heads)
        def _(i):
            query_copy(i).wait_send()
            g_high_copy(i).wait_send()
            delta_copy(i).wait_send()

            @pl.when(odd)
            def _():
                g_low_copy(i).wait_send()

            @pl.when(even)
            def _():
                near_copy(0, i).wait_send()

    wait_bytes(g_hbm.at[0, :, pl.ds(0, (parts - 1) * heads * HEAD_DIM)], g_send)
    for which in range(3):
        theirs = land.at[which, :, pl.ds(0, (parts - 1) * heads * HEAD_DIM)]
        wait_bytes(theirs, out_recv.at[which])
        wait_bytes(theirs, out_send.at[which])
        wait_bytes(land.at[which, :, pl.ds(0, heads * HEAD_DIM)], out_local.at[which])

    low = pl.ds(0, half * heads * HEAD_DIM)
    high = pl.ds(half * heads * HEAD_DIM, half * heads * HEAD_DIM)

    def summed(which, columns, far_at):
        total = land[which, :, columns].astype(jnp.float32) + land_far[far_at].astype(jnp.float32)
        return total.astype(jnp.bfloat16)

    wait_bytes(land_far.at[0], far_recv.at[0])
    out_q[0, :, low] = land[0, :, low]
    out_k[0, :, high] = land[1, :, high]
    out_v[0, :, high] = land[2, :, high]

    @pl.when(even)
    def _():
        out_q[0, :, high] = summed(0, high, 0)
        out_k[0, :, low] = land[1, :, low]
        out_v[0, :, low] = land[2, :, low]

    @pl.when(odd)
    def _():
        wait_bytes(land_far.at[1], far_recv.at[1])
        out_q[0, :, high] = land[0, :, high]
        out_k[0, :, low] = summed(1, low, 0)
        out_v[0, :, low] = summed(2, low, 1)


def on_device(query, key, value, output, grad_out, log_sum, group_length, cache_source):
    _, length, features = query.shape
    heads = features // HEAD_DIM
    per_head = (heads, length, HEAD_DIM)
    half = pltpu.VMEM(per_head, jnp.bfloat16)
    wide = pltpu.VMEM(per_head, jnp.float32)
    row = pltpu.VMEM((heads, 1, length), jnp.float32)
    dma = pltpu.SemaphoreType.DMA
    anywhere = pl.BlockSpec(memory_space=pl.ANY)
    smem = pl.BlockSpec(memory_space=pltpu.SMEM)
    vmem = pl.BlockSpec(memory_space=pltpu.VMEM)
    out = jax.ShapeDtypeStruct(grad_out.shape, jnp.bfloat16)
    flops = 10 * 2 * heads * length * length * HEAD_DIM
    return pl.pallas_call(
        kernel,
        out_shape=(out, out, out),
        in_specs=[smem, smem] + [anywhere] * 5 + [vmem],
        out_specs=(vmem, vmem, vmem),
        scratch_shapes=[
            half, half, half, half, half, half, half,
            pltpu.VMEM((heads, length), jnp.float32), row, row,
            wide, wide, wide,
            pltpu.VMEM((3,) + per_head, jnp.bfloat16), pltpu.VMEM((2,) + per_head, jnp.bfloat16),
            pltpu.VMEM((2,) + per_head, jnp.bfloat16),
            pltpu.VMEM((3,) + grad_out.shape[1:], jnp.bfloat16),
            pltpu.VMEM((2, grad_out.shape[1], grad_out.shape[2] // 2), jnp.bfloat16),
            dma((4, heads)), dma((heads,)), dma, dma((heads,)), dma((2,)), dma((2, heads)),
            dma((2, heads)), dma((2, heads)), dma, dma((2, heads)),
            dma((2, 2, heads)), dma((2,)), dma((2,)), dma((3,)), dma((3,)), dma((3,)),
        ],
        compiler_params=pltpu.CompilerParams(
            collective_id=0, has_side_effects=True, vmem_limit_bytes=60 * 1024 * 1024
        ),
        cost_estimate=pl.CostEstimate(
            flops=flops, bytes_accessed=8 * length * features * 2, transcendentals=2 * heads * length * length
        ),
        name="attention_backward",
    )(group_length, cache_source, query, key, value, output, grad_out, log_sum)


def solution(mesh):
    by_head, by_token = P("group", None, "head"), P("group", "head", None)
    return jax.shard_map(
        on_device,
        mesh=mesh,
        in_specs=(by_head, by_head, by_head, by_head, by_token, by_token, P(), P()),
        out_specs=(by_token, by_token, by_token),
        check_vma=False,
    )
```

```python
import functools
import math

import jax
import jax.numpy as jnp
from jax import lax
from jax.experimental import pallas as pl
from jax.experimental.pallas import tpu as pltpu
from jax.sharding import PartitionSpec as P

HEAD_DIM = 128
MESH = pl.DeviceIdType.MESH
SCALE = HEAD_DIM**-0.5
LOG2E = math.log2(math.e)
DEAD = 1e30


def dot_nt(a, b):
    return lax.dot_general(a, b, (((1,), (1,)), ((), ())), preferred_element_type=jnp.float32)


def dot_nn(a, b):
    return jnp.dot(a, b, preferred_element_type=jnp.float32)


def block_grads(q, g, lse_row, delta_row, k, kt, v):
    prob = jnp.exp2(dot_nt(k, q) * (SCALE * LOG2E) - lse_row)
    grad_score = (prob * (dot_nt(v, g) - delta_row)).astype(jnp.bfloat16)
    grad_v = dot_nn(prob.astype(jnp.bfloat16), g)
    grad_k = dot_nn(grad_score, q)
    grad_q = dot_nn(kt, grad_score).T
    return grad_q, grad_k, grad_v


def kernel(
    len_hbm, source_hbm, q_hbm, k_hbm, v_hbm, o_hbm, g_hbm, lse_hbm,
    out_q, out_k, out_v,
    len_ref, source_ref, q_own, k_own, v_own, o_own, g_own, moved_a, moved_b, lse_own, lse_next, delta_own, delta_next,
    acc_q, acc_k, acc_v, stage, cross_out, cross_in, land, land_far,
    load_sem, local_sem, g_send, g_recv, small_load, lse_sem, a_sem, b_sem, low_sem, direct_send, delta_sem,
    near_sem, far_send, far_recv, out_send, out_recv, out_local,
):
    heads, length, _ = q_own.shape
    groups = lax.axis_size("group")
    parts = lax.axis_size("head")
    half = parts // 2
    rows = length // parts
    group, me = lax.axis_index("group"), lax.axis_index("head")
    after, before = lax.rem(group + 1, groups), lax.rem(group + groups - 1, groups)
    even = lax.rem(group, 2) == 0
    odd = lax.rem(group, 2) == 1
    lower = me < half
    upper = me >= half
    near = lax.rem(group, 2) * before + (1 - lax.rem(group, 2)) * after
    far = lax.rem(group, 2) * after + (1 - lax.rem(group, 2)) * before

    def lanes(i):
        return pl.ds(pl.multiple_of(i * HEAD_DIM, HEAD_DIM), HEAD_DIM)

    def token_rows(part):
        return pl.ds(pl.multiple_of(part * rows, rows), rows)

    low_rows, high_rows = pl.ds(0, length // 2), pl.ds(length // 2, length // 2)

    def to(src, dst, send, recv, device):
        return pltpu.make_async_remote_copy(
            src_ref=src, dst_ref=dst, send_sem=send, recv_sem=recv,
            device_id=device, device_id_type=MESH,
        )

    def wait_bytes(ref, sem):
        pltpu.make_async_copy(ref, ref, sem).wait()

    def loads(i):
        pairs = ((k_hbm, k_own), (v_hbm, v_own), (q_hbm, q_own), (o_hbm, o_own))
        return [
            pltpu.make_async_copy(src.at[0, :, lanes(i)], dst.at[i], load_sem.at[at, i])
            for at, (src, dst) in enumerate(pairs)
        ]

    def local_g(i):
        return pltpu.make_async_copy(
            g_hbm.at[0, :, lanes(me * heads + i)], g_own.at[i, token_rows(me)], local_sem.at[i]
        )

    def key_copy(i):
        return to(k_hbm.at[0, :, lanes(i)], moved_a.at[i], a_sem.at[0, i], a_sem.at[1, i], (after, me))

    def value_copy(i):
        return to(v_hbm.at[0, :, lanes(i)], moved_b.at[i], b_sem.at[0, i], b_sem.at[1, i], (after, me))

    def query_copy(i):
        return to(q_hbm.at[0, :, lanes(i)], moved_a.at[i], a_sem.at[0, i], a_sem.at[1, i], (before, me))

    def g_high_copy(i):
        return to(
            g_own.at[i, high_rows], moved_b.at[i, high_rows], b_sem.at[0, i], b_sem.at[1, i], (before, me)
        )

    def g_low_copy(i):
        return to(
            g_own.at[i, low_rows], moved_b.at[i, low_rows], low_sem.at[0, i], low_sem.at[1, i], (before, me)
        )

    def delta_copy(i):
        return to(delta_own.at[i], delta_next.at[i], delta_sem.at[0, i], delta_sem.at[1, i], (before, me))

    def near_copy(which, i):
        return to(
            cross_out.at[which, i], cross_in.at[which, i],
            near_sem.at[0, which, i], near_sem.at[1, which, i], (near, me),
        )

    lse_copy = to(lse_hbm, lse_next, lse_sem.at[0], lse_sem.at[1], (before, me))

    small = ((lse_hbm, lse_own), (len_hbm, len_ref), (source_hbm, source_ref))
    small_loads = [pltpu.make_async_copy(src, dst, small_load.at[i]) for i, (src, dst) in enumerate(small)]
    for copy in small_loads:
        copy.start()
    barrier = pltpu.get_barrier_semaphore()

    @pl.loop(1, parts)
    def _(step):
        pl.semaphore_signal(
            barrier, inc=1, device_id=(group, lax.rem(me + step, parts)), device_id_type=MESH
        )

    @pl.loop(0, parts)
    def _(part):
        pl.semaphore_signal(barrier, inc=1, device_id=(far, part), device_id_type=MESH)

    pl.semaphore_signal(barrier, inc=1, device_id=(near, me), device_id_type=MESH)

    @pl.loop(0, heads)
    def _(i):
        local_g(i).start()
        for copy in loads(i):
            copy.start()

    pl.semaphore_wait(barrier, 2 * parts)

    @pl.loop(0, heads)
    def _(i):
        @pl.loop(1, parts)
        def _(step):
            peer = lax.rem(me + step, parts)
            to(
                g_hbm.at[0, :, lanes(peer * heads + i)], g_own.at[i, token_rows(me)],
                g_send, g_recv.at[i], (group, peer),
            ).start()

        @pl.when(even & lower)
        def _():
            @pl.loop(0, half)
            def _(step):
                peer = half + lax.rem(me + step, half)
                to(
                    g_hbm.at[0, :, lanes(peer * heads + i)], moved_b.at[i, token_rows(me)],
                    direct_send, low_sem.at[1, i], (before, peer),
                ).start()

        @pl.when(lower)
        def _():
            key_copy(i).start()
            value_copy(i).start()

        @pl.when(upper)
        def _():
            query_copy(i).start()

    for copy in small_loads:
        copy.wait()
    own_len, before_len = len_ref[group], len_ref[before]
    linked_len = jnp.where(source_ref[group] == before, own_len, 0)
    after_len = jnp.where(source_ref[after] == group, len_ref[after], 0)
    query_at = lax.broadcasted_iota(jnp.int32, (1, length), 1)
    key_at = lax.broadcasted_iota(jnp.int32, (length, HEAD_DIM), 0)
    zero = jnp.zeros((), jnp.bfloat16)

    def own_row(i, live):
        return jnp.where(query_at < live, lse_own[i] * LOG2E, DEAD)

    def live_keys(k, live):
        return jnp.where(key_at < live, k, zero)

    def half_rows(x, live):
        return jnp.where(key_at < live, x, 0.0).astype(jnp.bfloat16)

    def send_out(which, i):
        columns = lanes(me * heads + i)

        @pl.loop(1, parts)
        def _(step):
            peer = lax.rem(me + step, parts)
            to(
                stage.at[which, i, token_rows(peer)], land.at[which, :, columns],
                out_send.at[which], out_recv.at[which], (group, peer),
            ).start()

        pltpu.make_async_copy(
            stage.at[which, i, token_rows(me)], land.at[which, :, columns], out_local.at[which]
        ).start()

    def send_far(which, i):
        columns = lanes(lax.rem(me, half) * heads + i)

        @pl.loop(0, parts)
        def _(step):
            peer = lax.rem(me + step, parts)
            to(
                cross_out.at[which, i, token_rows(peer)], land_far.at[which, :, columns],
                far_send.at[which], far_recv.at[which], (far, peer),
            ).start()

    def wait_g(i):
        wait_bytes(g_own.at[i, pl.ds(0, (parts - 1) * rows)], g_recv.at[i])
        local_g(i).wait()

    def own_delta(i):
        product = g_own[i].astype(jnp.float32) * o_own[i].astype(jnp.float32)
        delta = jnp.sum(product.T, axis=0, keepdims=True)
        delta_own[i] = delta
        return delta

    def own_block(i, delta):
        k = live_keys(k_own[i], own_len)
        return block_grads(q_own[i], g_own[i], own_row(i, own_len), delta, k, k.T, v_own[i])

    @pl.when(lower)
    def _():
        def finish_keys(i):
            near_copy(0, i).wait_recv()
            stage[1, i] = (acc_k[i] + cross_in[0, i].astype(jnp.float32)).astype(jnp.bfloat16)
            send_out(1, i)
            near_copy(1, i).wait_recv()
            stage[2, i] = (acc_v[i] + cross_in[1, i].astype(jnp.float32)).astype(jnp.bfloat16)
            send_out(2, i)

        @pl.loop(0, heads)
        def _(i):
            wait_g(i)
            for copy in loads(i):
                copy.wait()
            grad_q, grad_k, grad_v = own_block(i, own_delta(i))
            acc_q[i] = grad_q
            grad_k = jnp.where(key_at < own_len, grad_k * SCALE, 0.0)
            grad_v = jnp.where(key_at < own_len, grad_v, 0.0)

            @pl.when(even)
            def _():
                acc_k[i] = grad_k
                acc_v[i] = grad_v

            @pl.when(odd)
            def _():
                stage[1, i] = grad_k.astype(jnp.bfloat16)
                send_out(1, i)
                stage[2, i] = grad_v.astype(jnp.bfloat16)
                send_out(2, i)

        @pl.loop(0, heads)
        def _(i):
            key_copy(i).wait_recv()
            value_copy(i).wait_recv()
            k = live_keys(moved_a[i], before_len)
            grad_q, grad_k, grad_v = block_grads(
                q_own[i], g_own[i], own_row(i, linked_len), delta_own[i], k, k.T, moved_b[i]
            )
            cross_out[0, i] = half_rows(grad_k * SCALE, before_len)
            cross_out[1, i] = half_rows(grad_v, before_len)

            @pl.when(odd)
            def _():
                near_copy(0, i).start()
                near_copy(1, i).start()

            @pl.when(even)
            def _():
                send_far(0, i)
                send_far(1, i)

            stage[0, i] = ((acc_q[i] + grad_q) * SCALE).astype(jnp.bfloat16)
            send_out(0, i)

            @pl.when(even & (i > 0))
            def _():
                finish_keys(i - 1)

        @pl.when(even)
        def _():
            finish_keys(heads - 1)
            wait_bytes(cross_out.at[0], far_send.at[0])
            wait_bytes(cross_out.at[1], far_send.at[1])
            wait_bytes(g_hbm.at[0, :, pl.ds(0, half * heads * HEAD_DIM)], direct_send)

        @pl.loop(0, heads)
        def _(i):
            key_copy(i).wait_send()
            value_copy(i).wait_send()

            @pl.when(odd)
            def _():
                near_copy(0, i).wait_send()
                near_copy(1, i).wait_send()

    @pl.when(upper)
    def _():
        lse_copy.start()

        def finish_query(i):
            near_copy(0, i).wait_recv()
            stage[0, i] = (acc_q[i] * SCALE + cross_in[0, i].astype(jnp.float32)).astype(jnp.bfloat16)
            send_out(0, i)

        @pl.loop(0, heads)
        def _(i):
            wait_g(i)
            g_high_copy(i).start()

            @pl.when(odd)
            def _():
                g_low_copy(i).start()

            for copy in loads(i):
                copy.wait()
            delta = own_delta(i)
            delta_copy(i).start()
            grad_q, grad_k, grad_v = own_block(i, delta)
            acc_k[i] = grad_k
            acc_v[i] = grad_v

            @pl.when(even)
            def _():
                stage[0, i] = (grad_q * SCALE).astype(jnp.bfloat16)
                send_out(0, i)

            @pl.when(odd)
            def _():
                acc_q[i] = grad_q

        lse_copy.wait_recv()

        @pl.loop(0, heads)
        def _(i):
            query_copy(i).wait_recv()
            g_high_copy(i).wait_recv()
            g_low_copy(i).wait_recv()
            delta_copy(i).wait_recv()
            lse_row = jnp.where(query_at < after_len, lse_next[i] * LOG2E, DEAD)
            k = live_keys(k_own[i], own_len)
            grad_q, grad_k, grad_v = block_grads(
                moved_a[i], moved_b[i], lse_row, delta_next[i], k, k.T, v_own[i]
            )
            cross_out[0, i] = (grad_q * SCALE).astype(jnp.bfloat16)

            @pl.when(even)
            def _():
                near_copy(0, i).start()

            @pl.when(odd)
            def _():
                send_far(0, i)

            stage[1, i] = half_rows((acc_k[i] + grad_k) * SCALE, own_len)
            send_out(1, i)
            stage[2, i] = half_rows(acc_v[i] + grad_v, own_len)
            send_out(2, i)

            @pl.when(odd & (i > 0))
            def _():
                finish_query(i - 1)

        @pl.when(odd)
        def _():
            finish_query(heads - 1)
            wait_bytes(cross_out.at[0], far_send.at[0])

        lse_copy.wait_send()

        @pl.loop(0, heads)
        def _(i):
            query_copy(i).wait_send()
            g_high_copy(i).wait_send()
            delta_copy(i).wait_send()

            @pl.when(odd)
            def _():
                g_low_copy(i).wait_send()

            @pl.when(even)
            def _():
                near_copy(0, i).wait_send()

    wait_bytes(g_hbm.at[0, :, pl.ds(0, (parts - 1) * heads * HEAD_DIM)], g_send)
    for which in range(3):
        theirs = land.at[which, :, pl.ds(0, (parts - 1) * heads * HEAD_DIM)]
        wait_bytes(theirs, out_recv.at[which])
        wait_bytes(theirs, out_send.at[which])
        wait_bytes(land.at[which, :, pl.ds(0, heads * HEAD_DIM)], out_local.at[which])

    low = pl.ds(0, half * heads * HEAD_DIM)
    high = pl.ds(half * heads * HEAD_DIM, half * heads * HEAD_DIM)

    def summed(which, columns, far_at):
        total = land[which, :, columns].astype(jnp.float32) + land_far[far_at].astype(jnp.float32)
        return total.astype(jnp.bfloat16)

    wait_bytes(land_far.at[0], far_recv.at[0])
    out_q[0, :, low] = land[0, :, low]
    out_k[0, :, high] = land[1, :, high]
    out_v[0, :, high] = land[2, :, high]

    @pl.when(even)
    def _():
        out_q[0, :, high] = summed(0, high, 0)
        out_k[0, :, low] = land[1, :, low]
        out_v[0, :, low] = land[2, :, low]

    @pl.when(odd)
    def _():
        wait_bytes(land_far.at[1], far_recv.at[1])
        out_q[0, :, high] = land[0, :, high]
        out_k[0, :, low] = summed(1, low, 0)
        out_v[0, :, low] = summed(2, low, 1)


def write_kernel(in_q, in_k, in_v, out_q, out_k, out_v, sems):
    pairs = ((in_q, out_q), (in_k, out_k), (in_v, out_v))
    copies = [pltpu.make_async_copy(src, dst, sems.at[i]) for i, (src, dst) in enumerate(pairs)]
    for copy in copies:
        copy.start()
    for copy in copies:
        copy.wait()


def on_device(query, key, value, output, grad_out, log_sum, group_length, cache_source):
    _, length, features = query.shape
    heads = features // HEAD_DIM
    per_head = (heads, length, HEAD_DIM)
    half = pltpu.VMEM(per_head, jnp.bfloat16)
    wide = pltpu.VMEM(per_head, jnp.float32)
    row = pltpu.VMEM((heads, 1, length), jnp.float32)
    dma = pltpu.SemaphoreType.DMA
    anywhere = pl.BlockSpec(memory_space=pl.ANY)
    vmem = pl.BlockSpec(memory_space=pltpu.VMEM)
    out = jax.ShapeDtypeStruct(grad_out.shape, jnp.bfloat16)
    flops = 10 * 2 * heads * length * length * HEAD_DIM
    rows_first = log_sum.transpose(1, 0, 2)
    inputs = (group_length, cache_source, query, key, value, output, grad_out, rows_first)
    landed = pl.pallas_call(
        kernel,
        out_shape=(out, out, out),
        in_specs=[anywhere] * 8,
        out_specs=(vmem, vmem, vmem),
        scratch_shapes=[
            pltpu.SMEM(group_length.shape, jnp.int32), pltpu.SMEM(cache_source.shape, jnp.int32),
            half, half, half, half, half, half, half,
            row, row, row, row,
            wide, wide, wide,
            pltpu.VMEM((3,) + per_head, jnp.bfloat16), pltpu.VMEM((2,) + per_head, jnp.bfloat16),
            pltpu.VMEM((2,) + per_head, jnp.bfloat16),
            pltpu.VMEM((3,) + grad_out.shape[1:], jnp.bfloat16),
            pltpu.VMEM((2, grad_out.shape[1], grad_out.shape[2] // 2), jnp.bfloat16),
            dma((4, heads)), dma((heads,)), dma, dma((heads,)), dma((3,)), dma((2,)), dma((2, heads)),
            dma((2, heads)), dma((2, heads)), dma, dma((2, heads)),
            dma((2, 2, heads)), dma((2,)), dma((2,)), dma((3,)), dma((3,)), dma((3,)),
        ],
        compiler_params=pltpu.CompilerParams(
            collective_id=0, has_side_effects=True, vmem_limit_bytes=40 * 1024 * 1024
        ),
        cost_estimate=pl.CostEstimate(
            flops=flops, bytes_accessed=8 * length * features * 2, transcendentals=2 * heads * length * length
        ),
        name="attention_backward",
    )(*[pltpu.with_memory_space_constraint(x, pltpu.HBM) for x in inputs])
    return pl.pallas_call(
        write_kernel,
        out_shape=(out, out, out),
        in_specs=[vmem] * 3,
        out_specs=(anywhere, anywhere, anywhere),
        scratch_shapes=[dma((3,))],
        cost_estimate=pl.CostEstimate(flops=0, bytes_accessed=6 * out.size * 2, transcendentals=0),
        compiler_params=pltpu.CompilerParams(vmem_limit_bytes=16 * 1024 * 1024),
        name="write_out",
    )(*landed)


def solution(mesh):
    by_head, by_token = P("group", None, "head"), P("group", "head", None)
    return jax.shard_map(
        on_device,
        mesh=mesh,
        in_specs=(by_head, by_head, by_head, by_head, by_token, by_token, P(), P()),
        out_specs=(by_token, by_token, by_token),
        check_vma=False,
    )
```

```python
import functools
import math

import jax
import jax.numpy as jnp
from jax import lax
from jax.experimental import pallas as pl
from jax.experimental.pallas import tpu as pltpu
from jax.sharding import PartitionSpec as P

HEAD_DIM = 128
MESH = pl.DeviceIdType.MESH
SCALE = HEAD_DIM**-0.5
LOG2E = math.log2(math.e)
DEAD = 1e30


def dot_nt(a, b):
    return lax.dot_general(a, b, (((1,), (1,)), ((), ())), preferred_element_type=jnp.float32)


def dot_nn(a, b):
    return jnp.dot(a, b, preferred_element_type=jnp.float32)


def block_grads(q, g, lse_row, delta_row, k, kt, v):
    prob = jnp.exp2(dot_nt(k, q) * (SCALE * LOG2E) - lse_row)
    grad_score = (prob * (dot_nt(v, g) - delta_row)).astype(jnp.bfloat16)
    grad_v = dot_nn(prob.astype(jnp.bfloat16), g)
    grad_k = dot_nn(grad_score, q)
    grad_q = dot_nn(kt, grad_score).T
    return grad_q, grad_k, grad_v


def kernel(
    len_hbm, source_hbm, q_hbm, k_hbm, v_hbm, o_hbm, g_hbm, lse_hbm,
    out_q, out_k, out_v,
    len_ref, source_ref, q_own, k_own, v_own, o_own, g_own, moved_a, moved_b, lse_own, lse_next, delta_own, delta_next,
    acc_q, acc_k, acc_v, stage, cross_out, cross_in, land_far,
    load_sem, local_sem, g_send, g_recv, small_load, lse_sem, a_sem, b_sem, low_sem, direct_send, delta_sem,
    near_sem, far_send, far_recv, out_send, out_recv, out_local, far_ready,
):
    heads, length, _ = q_own.shape
    outs = (out_q, out_k, out_v)
    groups = lax.axis_size("group")
    parts = lax.axis_size("head")
    half = parts // 2
    rows = length // parts
    group, me = lax.axis_index("group"), lax.axis_index("head")
    after, before = lax.rem(group + 1, groups), lax.rem(group + groups - 1, groups)
    even = lax.rem(group, 2) == 0
    odd = lax.rem(group, 2) == 1
    lower = me < half
    upper = me >= half
    has_before, has_after = group > 0, group < groups - 1
    has_far = has_before & has_after
    near = lax.rem(group, 2) * before + (1 - lax.rem(group, 2)) * after
    far = lax.rem(group, 2) * after + (1 - lax.rem(group, 2)) * before

    def lanes(i):
        return pl.ds(pl.multiple_of(i * HEAD_DIM, HEAD_DIM), HEAD_DIM)

    def token_rows(part):
        return pl.ds(pl.multiple_of(part * rows, rows), rows)

    low_rows, high_rows = pl.ds(0, length // 2), pl.ds(length // 2, length // 2)

    def to(src, dst, send, recv, device):
        return pltpu.make_async_remote_copy(
            src_ref=src, dst_ref=dst, send_sem=send, recv_sem=recv,
            device_id=device, device_id_type=MESH,
        )

    def wait_bytes(ref, sem):
        pltpu.make_async_copy(ref, ref, sem).wait()

    def loads(i):
        pairs = ((k_hbm, k_own), (v_hbm, v_own), (q_hbm, q_own), (o_hbm, o_own))
        return [
            pltpu.make_async_copy(src.at[0, :, lanes(i)], dst.at[i], load_sem.at[at, i])
            for at, (src, dst) in enumerate(pairs)
        ]

    def local_g(i):
        return pltpu.make_async_copy(
            g_hbm.at[0, :, lanes(me * heads + i)], g_own.at[i, token_rows(me)], local_sem.at[i]
        )

    def key_copy(i):
        return to(k_hbm.at[0, :, lanes(i)], moved_a.at[i], a_sem.at[0, i], a_sem.at[1, i], (after, me))

    def value_copy(i):
        return to(v_hbm.at[0, :, lanes(i)], moved_b.at[i], b_sem.at[0, i], b_sem.at[1, i], (after, me))

    def query_copy(i):
        return to(q_hbm.at[0, :, lanes(i)], moved_a.at[i], a_sem.at[0, i], a_sem.at[1, i], (before, me))

    def g_high_copy(i):
        return to(
            g_own.at[i, high_rows], moved_b.at[i, high_rows], b_sem.at[0, i], b_sem.at[1, i], (before, me)
        )

    def g_low_copy(i):
        return to(
            g_own.at[i, low_rows], moved_b.at[i, low_rows], low_sem.at[0, i], low_sem.at[1, i], (before, me)
        )

    def delta_copy(i):
        return to(delta_own.at[i], delta_next.at[i], delta_sem.at[0, i], delta_sem.at[1, i], (before, me))

    def near_copy(which, i):
        return to(
            cross_out.at[which, i], cross_in.at[which, i],
            near_sem.at[0, which, i], near_sem.at[1, which, i], (near, me),
        )

    lse_copy = to(lse_hbm, lse_next, lse_sem.at[0], lse_sem.at[1], (before, me))

    barrier = pltpu.get_barrier_semaphore()

    @pl.loop(1, parts)
    def _(step):
        pl.semaphore_signal(
            barrier, inc=1, device_id=(group, lax.rem(me + step, parts)), device_id_type=MESH
        )

    pl.semaphore_signal(barrier, inc=1, device_id=(near, me), device_id_type=MESH)

    def greet_far(sem):
        @pl.loop(0, parts)
        def _(part):
            pl.semaphore_signal(sem, inc=1, device_id=(far, part), device_id_type=MESH)

    @pl.when(odd & has_far)
    def _():
        pl.semaphore_wait(barrier, 2 * parts)
        greet_far(far_ready)

    @pl.when(even | jnp.logical_not(has_far))
    def _():
        pl.semaphore_wait(barrier, parts)

    @pl.when(even & has_far)
    def _():
        greet_far(barrier)

    @pl.loop(0, heads)
    def _(i):
        @pl.loop(1, parts)
        def _(step):
            peer = lax.rem(me + step, parts)
            to(
                g_hbm.at[0, :, lanes(peer * heads + i)], g_own.at[i, token_rows(me)],
                g_send, g_recv.at[i], (group, peer),
            ).start()

    @pl.when(even & has_far)
    def _():
        pl.semaphore_wait(far_ready, parts)

    @pl.loop(0, heads)
    def _(i):
        @pl.when(even & lower & has_before)
        def _():
            @pl.loop(0, half)
            def _(step):
                peer = half + lax.rem(me + step, half)
                to(
                    g_hbm.at[0, :, lanes(peer * heads + i)], moved_b.at[i, token_rows(me)],
                    direct_send, low_sem.at[1, i], (before, peer),
                ).start()

    @pl.loop(0, heads)
    def _(i):
        @pl.when(lower & has_after)
        def _():
            key_copy(i).start()
            value_copy(i).start()

        @pl.when(upper & has_before)
        def _():
            query_copy(i).start()

    small = ((lse_hbm, lse_own), (len_hbm, len_ref), (source_hbm, source_ref))
    small_loads = [pltpu.make_async_copy(src, dst, small_load.at[i]) for i, (src, dst) in enumerate(small)]
    for copy in small_loads:
        copy.start()
    @pl.loop(0, heads)
    def _(i):
        local_g(i).start()
        for copy in loads(i):
            copy.start()

    for copy in small_loads:
        copy.wait()
    own_len, before_len = len_ref[group], len_ref[before]
    linked_len = jnp.where(source_ref[group] == before, own_len, 0)
    after_len = jnp.where(source_ref[after] == group, len_ref[after], 0)
    query_at = lax.broadcasted_iota(jnp.int32, (1, length), 1)
    key_at = lax.broadcasted_iota(jnp.int32, (length, HEAD_DIM), 0)
    zero = jnp.zeros((), jnp.bfloat16)

    def own_row(i, live):
        return jnp.where(query_at < live, lse_own[i] * LOG2E, DEAD)

    def live_keys(k, live):
        return jnp.where(key_at < live, k, zero)

    def half_rows(x, live):
        return jnp.where(key_at < live, x, 0.0).astype(jnp.bfloat16)

    def send_out(which, i):
        columns = lanes(me * heads + i)

        @pl.loop(1, parts)
        def _(step):
            peer = lax.rem(me + step, parts)
            to(
                stage.at[which, i, token_rows(peer)], outs[which].at[0, :, columns],
                out_send.at[which], out_recv.at[which], (group, peer),
            ).start()

        pltpu.make_async_copy(
            stage.at[which, i, token_rows(me)], outs[which].at[0, :, columns], out_local.at[which]
        ).start()

    def send_far(which, i):
        columns = lanes(lax.rem(me, half) * heads + i)

        @pl.loop(0, parts)
        def _(step):
            peer = lax.rem(me + step, parts)
            to(
                cross_out.at[which, i, token_rows(peer)], land_far.at[which, :, columns],
                far_send.at[which], far_recv.at[which], (far, peer),
            ).start()

    def wait_g(i):
        wait_bytes(g_own.at[i, pl.ds(0, (parts - 1) * rows)], g_recv.at[i])
        local_g(i).wait()

    def own_delta(i):
        product = g_own[i].astype(jnp.float32) * o_own[i].astype(jnp.float32)
        delta = jnp.sum(product.T, axis=0, keepdims=True)
        delta_own[i] = delta
        return delta

    def own_block(i, delta):
        k = live_keys(k_own[i], own_len)
        return block_grads(q_own[i], g_own[i], own_row(i, own_len), delta, k, k.T, v_own[i])

    @pl.when(lower)
    def _():
        def finish_keys(i):
            near_copy(0, i).wait_recv()
            stage[1, i] = (acc_k[i] + cross_in[0, i].astype(jnp.float32)).astype(jnp.bfloat16)
            send_out(1, i)
            near_copy(1, i).wait_recv()
            stage[2, i] = (acc_v[i] + cross_in[1, i].astype(jnp.float32)).astype(jnp.bfloat16)
            send_out(2, i)

        @pl.loop(0, heads)
        def _(i):
            wait_g(i)
            for copy in loads(i):
                copy.wait()
            grad_q, grad_k, grad_v = own_block(i, own_delta(i))
            acc_q[i] = grad_q
            grad_k = jnp.where(key_at < own_len, grad_k * SCALE, 0.0)
            grad_v = jnp.where(key_at < own_len, grad_v, 0.0)

            @pl.when(even)
            def _():
                acc_k[i] = grad_k
                acc_v[i] = grad_v

            @pl.when(odd)
            def _():
                stage[1, i] = grad_k.astype(jnp.bfloat16)
                send_out(1, i)
                stage[2, i] = grad_v.astype(jnp.bfloat16)
                send_out(2, i)

        @pl.loop(0, heads)
        def _(i):
            @pl.when(has_before)
            def _():
                key_copy(i).wait_recv()
                value_copy(i).wait_recv()
                k = live_keys(moved_a[i], before_len)
                grad_q, grad_k, grad_v = block_grads(
                    q_own[i], g_own[i], own_row(i, linked_len), delta_own[i], k, k.T, moved_b[i]
                )
                cross_out[0, i] = half_rows(grad_k * SCALE, before_len)
                cross_out[1, i] = half_rows(grad_v, before_len)

                @pl.when(odd)
                def _():
                    near_copy(0, i).start()
                    near_copy(1, i).start()

                @pl.when(even)
                def _():
                    send_far(0, i)
                    send_far(1, i)

                stage[0, i] = ((acc_q[i] + grad_q) * SCALE).astype(jnp.bfloat16)

            @pl.when(jnp.logical_not(has_before))
            def _():
                stage[0, i] = (acc_q[i] * SCALE).astype(jnp.bfloat16)

            send_out(0, i)

            @pl.when(even & (i > 0))
            def _():
                finish_keys(i - 1)

        @pl.when(even)
        def _():
            finish_keys(heads - 1)

        @pl.when(even & has_before)
        def _():
            wait_bytes(cross_out.at[0], far_send.at[0])
            wait_bytes(cross_out.at[1], far_send.at[1])
            wait_bytes(g_hbm.at[0, :, pl.ds(0, half * heads * HEAD_DIM)], direct_send)

        @pl.loop(0, heads)
        def _(i):
            @pl.when(has_after)
            def _():
                key_copy(i).wait_send()
                value_copy(i).wait_send()

            @pl.when(odd)
            def _():
                near_copy(0, i).wait_send()
                near_copy(1, i).wait_send()

    @pl.when(upper)
    def _():
        @pl.when(has_before)
        def _():
            lse_copy.start()

        def finish_query(i):
            near_copy(0, i).wait_recv()
            stage[0, i] = (acc_q[i] * SCALE + cross_in[0, i].astype(jnp.float32)).astype(jnp.bfloat16)
            send_out(0, i)

        @pl.loop(0, heads)
        def _(i):
            wait_g(i)
            @pl.when(has_before)
            def _():
                g_high_copy(i).start()

            @pl.when(odd)
            def _():
                g_low_copy(i).start()

            for copy in loads(i):
                copy.wait()
            delta = own_delta(i)

            @pl.when(has_before)
            def _():
                delta_copy(i).start()

            grad_q, grad_k, grad_v = own_block(i, delta)
            acc_k[i] = grad_k
            acc_v[i] = grad_v

            @pl.when(even)
            def _():
                stage[0, i] = (grad_q * SCALE).astype(jnp.bfloat16)
                send_out(0, i)

            @pl.when(odd)
            def _():
                acc_q[i] = grad_q

        @pl.when(has_after)
        def _():
            lse_copy.wait_recv()

        @pl.loop(0, heads)
        def _(i):
            @pl.when(has_after)
            def _():
                query_copy(i).wait_recv()
                g_high_copy(i).wait_recv()
                g_low_copy(i).wait_recv()
                delta_copy(i).wait_recv()
                lse_row = jnp.where(query_at < after_len, lse_next[i] * LOG2E, DEAD)
                k = live_keys(k_own[i], own_len)
                grad_q, grad_k, grad_v = block_grads(
                    moved_a[i], moved_b[i], lse_row, delta_next[i], k, k.T, v_own[i]
                )
                cross_out[0, i] = (grad_q * SCALE).astype(jnp.bfloat16)

                @pl.when(even)
                def _():
                    near_copy(0, i).start()

                @pl.when(odd)
                def _():
                    send_far(0, i)

                stage[1, i] = half_rows((acc_k[i] + grad_k) * SCALE, own_len)
                stage[2, i] = half_rows(acc_v[i] + grad_v, own_len)

            @pl.when(jnp.logical_not(has_after))
            def _():
                stage[1, i] = half_rows(acc_k[i] * SCALE, own_len)
                stage[2, i] = half_rows(acc_v[i], own_len)

            send_out(1, i)
            send_out(2, i)

            @pl.when(odd & (i > 0))
            def _():
                finish_query(i - 1)

        @pl.when(odd)
        def _():
            finish_query(heads - 1)

        @pl.when(odd & has_after)
        def _():
            wait_bytes(cross_out.at[0], far_send.at[0])

        @pl.when(has_before)
        def _():
            lse_copy.wait_send()

        @pl.loop(0, heads)
        def _(i):
            @pl.when(has_before)
            def _():
                query_copy(i).wait_send()
                g_high_copy(i).wait_send()
                delta_copy(i).wait_send()

            @pl.when(odd)
            def _():
                g_low_copy(i).wait_send()

            @pl.when(even)
            def _():
                near_copy(0, i).wait_send()

    wait_bytes(g_hbm.at[0, :, pl.ds(0, (parts - 1) * heads * HEAD_DIM)], g_send)
    for which in range(3):
        theirs = outs[which].at[0, :, pl.ds(0, (parts - 1) * heads * HEAD_DIM)]
        wait_bytes(theirs, out_recv.at[which])
        wait_bytes(theirs, out_send.at[which])
        wait_bytes(outs[which].at[0, :, pl.ds(0, heads * HEAD_DIM)], out_local.at[which])

    low = pl.ds(0, half * heads * HEAD_DIM)
    high = pl.ds(half * heads * HEAD_DIM, half * heads * HEAD_DIM)

    def add_far(out, columns, far_at):
        total = out[0, :, columns].astype(jnp.float32) + land_far[far_at].astype(jnp.float32)
        out[0, :, columns] = total.astype(jnp.bfloat16)

    @pl.when(has_far)
    def _():
        wait_bytes(land_far.at[0], far_recv.at[0])

    @pl.when(even & has_far)
    def _():
        add_far(out_q, high, 0)

    @pl.when(odd & has_far)
    def _():
        wait_bytes(land_far.at[1], far_recv.at[1])
        add_far(out_k, low, 0)
        add_far(out_v, low, 1)


def write_kernel(in_q, in_k, in_v, out_q, out_k, out_v, sems):
    pairs = ((in_q, out_q), (in_k, out_k), (in_v, out_v))
    copies = [pltpu.make_async_copy(src, dst, sems.at[i]) for i, (src, dst) in enumerate(pairs)]
    for copy in copies:
        copy.start()
    for copy in copies:
        copy.wait()


def on_device(query, key, value, output, grad_out, log_sum, group_length, cache_source):
    _, length, features = query.shape
    heads = features // HEAD_DIM
    per_head = (heads, length, HEAD_DIM)
    half = pltpu.VMEM(per_head, jnp.bfloat16)
    wide = pltpu.VMEM(per_head, jnp.float32)
    row = pltpu.VMEM((heads, 1, length), jnp.float32)
    dma = pltpu.SemaphoreType.DMA
    anywhere = pl.BlockSpec(memory_space=pl.ANY)
    vmem = pl.BlockSpec(memory_space=pltpu.VMEM)
    out = jax.ShapeDtypeStruct(grad_out.shape, jnp.bfloat16)
    flops = 10 * 2 * heads * length * length * HEAD_DIM
    rows_first = log_sum.transpose(1, 0, 2)
    inputs = (group_length, cache_source, query, key, value, output, grad_out, rows_first)
    landed = pl.pallas_call(
        kernel,
        out_shape=(out, out, out),
        in_specs=[anywhere] * 8,
        out_specs=(vmem, vmem, vmem),
        scratch_shapes=[
            pltpu.SMEM(group_length.shape, jnp.int32), pltpu.SMEM(cache_source.shape, jnp.int32),
            half, half, half, half, half, half, half,
            row, row, row, row,
            wide, wide, wide,
            pltpu.VMEM((3,) + per_head, jnp.bfloat16), pltpu.VMEM((2,) + per_head, jnp.bfloat16),
            pltpu.VMEM((2,) + per_head, jnp.bfloat16),
            pltpu.VMEM((2, grad_out.shape[1], grad_out.shape[2] // 2), jnp.bfloat16),
            dma((4, heads)), dma((heads,)), dma, dma((heads,)), dma((3,)), dma((2,)), dma((2, heads)),
            dma((2, heads)), dma((2, heads)), dma, dma((2, heads)),
            dma((2, 2, heads)), dma((2,)), dma((2,)), dma((3,)), dma((3,)), dma((3,)),
            pltpu.SemaphoreType.REGULAR,
        ],
        compiler_params=pltpu.CompilerParams(
            collective_id=0, has_side_effects=True, vmem_limit_bytes=40 * 1024 * 1024
        ),
        cost_estimate=pl.CostEstimate(
            flops=flops, bytes_accessed=8 * length * features * 2, transcendentals=2 * heads * length * length
        ),
        name="attention_backward",
    )(*[pltpu.with_memory_space_constraint(x, pltpu.HBM) for x in inputs])
    return pl.pallas_call(
        write_kernel,
        out_shape=(out, out, out),
        in_specs=[vmem] * 3,
        out_specs=(anywhere, anywhere, anywhere),
        scratch_shapes=[dma((3,))],
        cost_estimate=pl.CostEstimate(flops=0, bytes_accessed=6 * out.size * 2, transcendentals=0),
        compiler_params=pltpu.CompilerParams(vmem_limit_bytes=16 * 1024 * 1024),
        name="write_out",
    )(*landed)


def solution(mesh):
    by_head, by_token = P("group", None, "head"), P("group", "head", None)
    return jax.shard_map(
        on_device,
        mesh=mesh,
        in_specs=(by_head, by_head, by_head, by_head, by_token, by_token, P(), P()),
        out_specs=(by_token, by_token, by_token),
        check_vma=False,
    )
```

```python
import functools
import math

import jax
import jax.numpy as jnp
from jax import lax
from jax.experimental import pallas as pl
from jax.experimental.pallas import tpu as pltpu
from jax.sharding import PartitionSpec as P

HEAD_DIM = 128
MESH = pl.DeviceIdType.MESH
SCALE = HEAD_DIM**-0.5
LOG2E = math.log2(math.e)
DEAD = 1e30


def dot_nt(a, b):
    return lax.dot_general(a, b, (((1,), (1,)), ((), ())), preferred_element_type=jnp.float32)


def dot_nn(a, b):
    return jnp.dot(a, b, preferred_element_type=jnp.float32)


def block_grads(q, g, lse_row, delta_row, k, kt, v):
    prob = jnp.exp2(dot_nt(k, q) * (SCALE * LOG2E) - lse_row)
    grad_score = (prob * (dot_nt(v, g) - delta_row)).astype(jnp.bfloat16)
    grad_v = dot_nn(prob.astype(jnp.bfloat16), g)
    grad_k = dot_nn(grad_score, q)
    grad_q = dot_nn(kt, grad_score).T
    return grad_q, grad_k, grad_v


def kernel(
    len_hbm, source_hbm, q_hbm, k_hbm, v_hbm, o_hbm, g_hbm, lse_hbm,
    out_q, out_k, out_v,
    len_ref, source_ref, q_own, k_own, v_own, o_own, g_own, moved_a, moved_b, lse_own, lse_next, delta_own, delta_next,
    acc_q, acc_k, acc_v, stage, cross_out, cross_in, land_far,
    load_sem, local_sem, g_send, g_recv, small_load, lse_sem, a_sem, b_sem, low_sem, direct_send, delta_sem,
    near_sem, far_send, far_recv, out_send, out_recv, out_local, far_ready,
):
    heads, length, _ = q_own.shape
    outs = (out_q, out_k, out_v)
    groups = lax.axis_size("group")
    parts = lax.axis_size("head")
    half = parts // 2
    rows = length // parts
    group, me = lax.axis_index("group"), lax.axis_index("head")
    after, before = lax.rem(group + 1, groups), lax.rem(group + groups - 1, groups)
    even = lax.rem(group, 2) == 0
    odd = lax.rem(group, 2) == 1
    lower = me < half
    upper = me >= half
    has_before, has_after = group > 0, group < groups - 1
    has_far = has_before & has_after
    chip_at = lax.rem((group - lax.rem(group + 1, 2) * 2 + groups) // 2, 4)
    first = (odd & (chip_at < 3)) | (even & (chip_at >= 3))
    second = (odd & (chip_at >= 3)) | (even & (chip_at < 3))
    near = lax.rem(group, 2) * before + (1 - lax.rem(group, 2)) * after
    far = lax.rem(group, 2) * after + (1 - lax.rem(group, 2)) * before

    def lanes(i):
        return pl.ds(pl.multiple_of(i * HEAD_DIM, HEAD_DIM), HEAD_DIM)

    def token_rows(part):
        return pl.ds(pl.multiple_of(part * rows, rows), rows)

    low_rows, high_rows = pl.ds(0, length // 2), pl.ds(length // 2, length // 2)

    def to(src, dst, send, recv, device):
        return pltpu.make_async_remote_copy(
            src_ref=src, dst_ref=dst, send_sem=send, recv_sem=recv,
            device_id=device, device_id_type=MESH,
        )

    def wait_bytes(ref, sem):
        pltpu.make_async_copy(ref, ref, sem).wait()

    def loads(i):
        pairs = ((k_hbm, k_own), (v_hbm, v_own), (q_hbm, q_own), (o_hbm, o_own))
        return [
            pltpu.make_async_copy(src.at[0, :, lanes(i)], dst.at[i], load_sem.at[at, i])
            for at, (src, dst) in enumerate(pairs)
        ]

    def local_g(i):
        return pltpu.make_async_copy(
            g_hbm.at[0, :, lanes(me * heads + i)], g_own.at[i, token_rows(me)], local_sem.at[i]
        )

    def key_copy(i):
        return to(k_hbm.at[0, :, lanes(i)], moved_a.at[i], a_sem.at[0, i], a_sem.at[1, i], (after, me))

    def value_copy(i):
        return to(v_hbm.at[0, :, lanes(i)], moved_b.at[i], b_sem.at[0, i], b_sem.at[1, i], (after, me))

    def query_copy(i):
        return to(q_hbm.at[0, :, lanes(i)], moved_a.at[i], a_sem.at[0, i], a_sem.at[1, i], (before, me))

    def g_high_copy(i):
        return to(
            g_own.at[i, high_rows], moved_b.at[i, high_rows], b_sem.at[0, i], b_sem.at[1, i], (before, me)
        )

    def g_low_copy(i):
        return to(
            g_own.at[i, low_rows], moved_b.at[i, low_rows], low_sem.at[0, i], low_sem.at[1, i], (before, me)
        )

    def delta_copy(i):
        return to(delta_own.at[i], delta_next.at[i], delta_sem.at[0, i], delta_sem.at[1, i], (before, me))

    def near_copy(which, i):
        return to(
            cross_out.at[which, i], cross_in.at[which, i],
            near_sem.at[0, which, i], near_sem.at[1, which, i], (near, me),
        )

    lse_copy = to(lse_hbm, lse_next, lse_sem.at[0], lse_sem.at[1], (before, me))

    barrier = pltpu.get_barrier_semaphore()

    @pl.loop(1, parts)
    def _(step):
        pl.semaphore_signal(
            barrier, inc=1, device_id=(group, lax.rem(me + step, parts)), device_id_type=MESH
        )

    pl.semaphore_signal(barrier, inc=1, device_id=(near, me), device_id_type=MESH)

    def greet_far(sem):
        @pl.loop(0, parts)
        def _(part):
            pl.semaphore_signal(sem, inc=1, device_id=(far, part), device_id_type=MESH)

    @pl.when(second & has_far)
    def _():
        pl.semaphore_wait(barrier, 2 * parts)
        greet_far(far_ready)

    @pl.when(first | jnp.logical_not(has_far))
    def _():
        pl.semaphore_wait(barrier, parts)

    @pl.when(first & has_far)
    def _():
        greet_far(barrier)

    @pl.loop(0, heads)
    def _(i):
        @pl.loop(1, parts)
        def _(step):
            peer = lax.rem(me + step, parts)
            to(
                g_hbm.at[0, :, lanes(peer * heads + i)], g_own.at[i, token_rows(me)],
                g_send, g_recv.at[i], (group, peer),
            ).start()

    @pl.when(first & has_far)
    def _():
        pl.semaphore_wait(far_ready, parts)

    @pl.loop(0, heads)
    def _(i):
        @pl.when(even & lower & has_before)
        def _():
            @pl.loop(0, half)
            def _(step):
                peer = half + lax.rem(me + step, half)
                to(
                    g_hbm.at[0, :, lanes(peer * heads + i)], moved_b.at[i, token_rows(me)],
                    direct_send, low_sem.at[1, i], (before, peer),
                ).start()

    @pl.loop(0, heads)
    def _(i):
        @pl.when(lower & has_after)
        def _():
            key_copy(i).start()
            value_copy(i).start()

        @pl.when(upper & has_before)
        def _():
            query_copy(i).start()

    small = ((lse_hbm, lse_own), (len_hbm, len_ref), (source_hbm, source_ref))
    small_loads = [pltpu.make_async_copy(src, dst, small_load.at[i]) for i, (src, dst) in enumerate(small)]
    for copy in small_loads:
        copy.start()
    @pl.loop(0, heads)
    def _(i):
        local_g(i).start()
        for copy in loads(i):
            copy.start()

    for copy in small_loads:
        copy.wait()
    own_len, before_len = len_ref[group], len_ref[before]
    linked_len = jnp.where(source_ref[group] == before, own_len, 0)
    after_len = jnp.where(source_ref[after] == group, len_ref[after], 0)
    query_at = lax.broadcasted_iota(jnp.int32, (1, length), 1)
    key_at = lax.broadcasted_iota(jnp.int32, (length, HEAD_DIM), 0)
    zero = jnp.zeros((), jnp.bfloat16)

    def own_row(i, live):
        return jnp.where(query_at < live, lse_own[i] * LOG2E, DEAD)

    def live_keys(k, live):
        return jnp.where(key_at < live, k, zero)

    def half_rows(x, live):
        return jnp.where(key_at < live, x, 0.0).astype(jnp.bfloat16)

    def send_out(which, i):
        columns = lanes(me * heads + i)

        @pl.loop(1, parts)
        def _(step):
            peer = lax.rem(me + step, parts)
            to(
                stage.at[which, i, token_rows(peer)], outs[which].at[0, :, columns],
                out_send.at[which], out_recv.at[which], (group, peer),
            ).start()

        pltpu.make_async_copy(
            stage.at[which, i, token_rows(me)], outs[which].at[0, :, columns], out_local.at[which]
        ).start()

    def send_far(which, i):
        columns = lanes(lax.rem(me, half) * heads + i)

        @pl.loop(0, parts)
        def _(step):
            peer = lax.rem(me + step, parts)
            to(
                cross_out.at[which, i, token_rows(peer)], land_far.at[which, :, columns],
                far_send.at[which], far_recv.at[which], (far, peer),
            ).start()

    def wait_g(i):
        wait_bytes(g_own.at[i, pl.ds(0, (parts - 1) * rows)], g_recv.at[i])
        local_g(i).wait()

    def own_delta(i):
        product = g_own[i].astype(jnp.float32) * o_own[i].astype(jnp.float32)
        delta = jnp.sum(product.T, axis=0, keepdims=True)
        delta_own[i] = delta
        return delta

    def own_block(i, delta):
        k = live_keys(k_own[i], own_len)
        return block_grads(q_own[i], g_own[i], own_row(i, own_len), delta, k, k.T, v_own[i])

    @pl.when(lower)
    def _():
        def finish_keys(i):
            near_copy(0, i).wait_recv()
            stage[1, i] = (acc_k[i] + cross_in[0, i].astype(jnp.float32)).astype(jnp.bfloat16)
            send_out(1, i)
            near_copy(1, i).wait_recv()
            stage[2, i] = (acc_v[i] + cross_in[1, i].astype(jnp.float32)).astype(jnp.bfloat16)
            send_out(2, i)

        @pl.loop(0, heads)
        def _(i):
            wait_g(i)
            for copy in loads(i):
                copy.wait()
            grad_q, grad_k, grad_v = own_block(i, own_delta(i))
            acc_q[i] = grad_q
            grad_k = jnp.where(key_at < own_len, grad_k * SCALE, 0.0)
            grad_v = jnp.where(key_at < own_len, grad_v, 0.0)

            @pl.when(even)
            def _():
                acc_k[i] = grad_k
                acc_v[i] = grad_v

            @pl.when(odd)
            def _():
                stage[1, i] = grad_k.astype(jnp.bfloat16)
                send_out(1, i)
                stage[2, i] = grad_v.astype(jnp.bfloat16)
                send_out(2, i)

        @pl.loop(0, heads)
        def _(i):
            @pl.when(has_before)
            def _():
                key_copy(i).wait_recv()
                value_copy(i).wait_recv()
                k = live_keys(moved_a[i], before_len)
                grad_q, grad_k, grad_v = block_grads(
                    q_own[i], g_own[i], own_row(i, linked_len), delta_own[i], k, k.T, moved_b[i]
                )
                cross_out[0, i] = half_rows(grad_k * SCALE, before_len)
                cross_out[1, i] = half_rows(grad_v, before_len)

                @pl.when(odd)
                def _():
                    near_copy(0, i).start()
                    near_copy(1, i).start()

                @pl.when(even)
                def _():
                    send_far(0, i)
                    send_far(1, i)

                stage[0, i] = ((acc_q[i] + grad_q) * SCALE).astype(jnp.bfloat16)

            @pl.when(jnp.logical_not(has_before))
            def _():
                stage[0, i] = (acc_q[i] * SCALE).astype(jnp.bfloat16)

            send_out(0, i)

            @pl.when(even & (i > 0))
            def _():
                finish_keys(i - 1)

        @pl.when(even)
        def _():
            finish_keys(heads - 1)

        @pl.when(even & has_before)
        def _():
            wait_bytes(cross_out.at[0], far_send.at[0])
            wait_bytes(cross_out.at[1], far_send.at[1])
            wait_bytes(g_hbm.at[0, :, pl.ds(0, half * heads * HEAD_DIM)], direct_send)

        @pl.loop(0, heads)
        def _(i):
            @pl.when(has_after)
            def _():
                key_copy(i).wait_send()
                value_copy(i).wait_send()

            @pl.when(odd)
            def _():
                near_copy(0, i).wait_send()
                near_copy(1, i).wait_send()

    @pl.when(upper)
    def _():
        @pl.when(has_before)
        def _():
            lse_copy.start()

        def finish_query(i):
            near_copy(0, i).wait_recv()
            stage[0, i] = (acc_q[i] * SCALE + cross_in[0, i].astype(jnp.float32)).astype(jnp.bfloat16)
            send_out(0, i)

        @pl.loop(0, heads)
        def _(i):
            wait_g(i)
            @pl.when(has_before)
            def _():
                g_high_copy(i).start()

            @pl.when(odd)
            def _():
                g_low_copy(i).start()

            for copy in loads(i):
                copy.wait()
            delta = own_delta(i)

            @pl.when(has_before)
            def _():
                delta_copy(i).start()

            grad_q, grad_k, grad_v = own_block(i, delta)
            acc_k[i] = grad_k
            acc_v[i] = grad_v

            @pl.when(even)
            def _():
                stage[0, i] = (grad_q * SCALE).astype(jnp.bfloat16)
                send_out(0, i)

            @pl.when(odd)
            def _():
                acc_q[i] = grad_q

        @pl.when(has_after)
        def _():
            lse_copy.wait_recv()

        @pl.loop(0, heads)
        def _(i):
            @pl.when(has_after)
            def _():
                query_copy(i).wait_recv()
                g_high_copy(i).wait_recv()
                g_low_copy(i).wait_recv()
                delta_copy(i).wait_recv()
                lse_row = jnp.where(query_at < after_len, lse_next[i] * LOG2E, DEAD)
                k = live_keys(k_own[i], own_len)
                grad_q, grad_k, grad_v = block_grads(
                    moved_a[i], moved_b[i], lse_row, delta_next[i], k, k.T, v_own[i]
                )
                cross_out[0, i] = (grad_q * SCALE).astype(jnp.bfloat16)

                @pl.when(even)
                def _():
                    near_copy(0, i).start()

                @pl.when(odd)
                def _():
                    send_far(0, i)

                stage[1, i] = half_rows((acc_k[i] + grad_k) * SCALE, own_len)
                stage[2, i] = half_rows(acc_v[i] + grad_v, own_len)

            @pl.when(jnp.logical_not(has_after))
            def _():
                stage[1, i] = half_rows(acc_k[i] * SCALE, own_len)
                stage[2, i] = half_rows(acc_v[i], own_len)

            send_out(1, i)
            send_out(2, i)

            @pl.when(odd & (i > 0))
            def _():
                finish_query(i - 1)

        @pl.when(odd)
        def _():
            finish_query(heads - 1)

        @pl.when(odd & has_after)
        def _():
            wait_bytes(cross_out.at[0], far_send.at[0])

        @pl.when(has_before)
        def _():
            lse_copy.wait_send()

        @pl.loop(0, heads)
        def _(i):
            @pl.when(has_before)
            def _():
                query_copy(i).wait_send()
                g_high_copy(i).wait_send()
                delta_copy(i).wait_send()

            @pl.when(odd)
            def _():
                g_low_copy(i).wait_send()

            @pl.when(even)
            def _():
                near_copy(0, i).wait_send()

    wait_bytes(g_hbm.at[0, :, pl.ds(0, (parts - 1) * heads * HEAD_DIM)], g_send)
    for which in range(3):
        theirs = outs[which].at[0, :, pl.ds(0, (parts - 1) * heads * HEAD_DIM)]
        wait_bytes(theirs, out_recv.at[which])
        wait_bytes(theirs, out_send.at[which])
        wait_bytes(outs[which].at[0, :, pl.ds(0, heads * HEAD_DIM)], out_local.at[which])

    low = pl.ds(0, half * heads * HEAD_DIM)
    high = pl.ds(half * heads * HEAD_DIM, half * heads * HEAD_DIM)

    def add_far(out, columns, far_at):
        total = out[0, :, columns].astype(jnp.float32) + land_far[far_at].astype(jnp.float32)
        out[0, :, columns] = total.astype(jnp.bfloat16)

    @pl.when(has_far)
    def _():
        wait_bytes(land_far.at[0], far_recv.at[0])

    @pl.when(even & has_far)
    def _():
        add_far(out_q, high, 0)

    @pl.when(odd & has_far)
    def _():
        wait_bytes(land_far.at[1], far_recv.at[1])
        add_far(out_k, low, 0)
        add_far(out_v, low, 1)


def write_kernel(in_q, in_k, in_v, out_q, out_k, out_v, sems):
    pairs = ((in_q, out_q), (in_k, out_k), (in_v, out_v))
    copies = [pltpu.make_async_copy(src, dst, sems.at[i]) for i, (src, dst) in enumerate(pairs)]
    for copy in copies:
        copy.start()
    for copy in copies:
        copy.wait()


def on_device(query, key, value, output, grad_out, log_sum, group_length, cache_source):
    _, length, features = query.shape
    heads = features // HEAD_DIM
    per_head = (heads, length, HEAD_DIM)
    half = pltpu.VMEM(per_head, jnp.bfloat16)
    wide = pltpu.VMEM(per_head, jnp.float32)
    row = pltpu.VMEM((heads, 1, length), jnp.float32)
    dma = pltpu.SemaphoreType.DMA
    anywhere = pl.BlockSpec(memory_space=pl.ANY)
    vmem = pl.BlockSpec(memory_space=pltpu.VMEM)
    out = jax.ShapeDtypeStruct(grad_out.shape, jnp.bfloat16)
    flops = 10 * 2 * heads * length * length * HEAD_DIM
    rows_first = log_sum.transpose(1, 0, 2)
    inputs = (group_length, cache_source, query, key, value, output, grad_out, rows_first)
    landed = pl.pallas_call(
        kernel,
        out_shape=(out, out, out),
        in_specs=[anywhere] * 8,
        out_specs=(vmem, vmem, vmem),
        scratch_shapes=[
            pltpu.SMEM(group_length.shape, jnp.int32), pltpu.SMEM(cache_source.shape, jnp.int32),
            half, half, half, half, half, half, half,
            row, row, row, row,
            wide, wide, wide,
            pltpu.VMEM((3,) + per_head, jnp.bfloat16), pltpu.VMEM((2,) + per_head, jnp.bfloat16),
            pltpu.VMEM((2,) + per_head, jnp.bfloat16),
            pltpu.VMEM((2, grad_out.shape[1], grad_out.shape[2] // 2), jnp.bfloat16),
            dma((4, heads)), dma((heads,)), dma, dma((heads,)), dma((3,)), dma((2,)), dma((2, heads)),
            dma((2, heads)), dma((2, heads)), dma, dma((2, heads)),
            dma((2, 2, heads)), dma((2,)), dma((2,)), dma((3,)), dma((3,)), dma((3,)),
            pltpu.SemaphoreType.REGULAR,
        ],
        compiler_params=pltpu.CompilerParams(
            collective_id=0, has_side_effects=True, vmem_limit_bytes=40 * 1024 * 1024
        ),
        cost_estimate=pl.CostEstimate(
            flops=flops, bytes_accessed=8 * length * features * 2, transcendentals=2 * heads * length * length
        ),
        name="attention_backward",
    )(*[pltpu.with_memory_space_constraint(x, pltpu.HBM) for x in inputs])
    return pl.pallas_call(
        write_kernel,
        out_shape=(out, out, out),
        in_specs=[vmem] * 3,
        out_specs=(anywhere, anywhere, anywhere),
        scratch_shapes=[dma((3,))],
        cost_estimate=pl.CostEstimate(flops=0, bytes_accessed=6 * out.size * 2, transcendentals=0),
        compiler_params=pltpu.CompilerParams(vmem_limit_bytes=16 * 1024 * 1024),
        name="write_out",
    )(*landed)


def solution(mesh):
    by_head, by_token = P("group", None, "head"), P("group", "head", None)
    return jax.shard_map(
        on_device,
        mesh=mesh,
        in_specs=(by_head, by_head, by_head, by_head, by_token, by_token, P(), P()),
        out_specs=(by_token, by_token, by_token),
        check_vma=False,
    )
```

```python
import functools
import math

import jax
import jax.numpy as jnp
from jax import lax
from jax.experimental import pallas as pl
from jax.experimental.pallas import tpu as pltpu
from jax.sharding import PartitionSpec as P

HEAD_DIM = 128
MESH = pl.DeviceIdType.MESH
SCALE = HEAD_DIM**-0.5
LOG2E = math.log2(math.e)
DEAD = 1e30


def dot_nt(a, b):
    return lax.dot_general(a, b, (((1,), (1,)), ((), ())), preferred_element_type=jnp.float32)


def dot_nn(a, b):
    return jnp.dot(a, b, preferred_element_type=jnp.float32)


def block_grads(q, g, lse_row, delta_row, k, kt, v):
    prob = jnp.exp2(dot_nt(k, q) * (SCALE * LOG2E) - lse_row)
    grad_score = (prob * (dot_nt(v, g) - delta_row)).astype(jnp.bfloat16)
    grad_v = dot_nn(prob.astype(jnp.bfloat16), g)
    grad_k = dot_nn(grad_score, q)
    grad_q = dot_nn(kt, grad_score).T
    return grad_q, grad_k, grad_v


def kernel(
    len_hbm, source_hbm, q_hbm, k_hbm, v_hbm, o_hbm, g_hbm, lse_hbm,
    out_q, out_k, out_v,
    len_ref, source_ref, q_own, k_own, v_own, o_own, g_own, moved_a, moved_b, lse_own, lse_next, delta_own, delta_next,
    acc_q, acc_k, acc_v, stage, cross_out, cross_in, land_far,
    load_sem, local_sem, g_send, g_recv, small_load, lse_sem, a_sem, b_sem, low_sem, direct_send, delta_sem,
    near_sem, far_send, far_recv, out_send, out_recv, out_local, far_ready,
):
    heads, length, _ = q_own.shape
    outs = (out_q, out_k, out_v)
    groups = lax.axis_size("group")
    parts = lax.axis_size("head")
    half = parts // 2
    rows = length // parts
    group, me = lax.axis_index("group"), lax.axis_index("head")
    after, before = lax.rem(group + 1, groups), lax.rem(group + groups - 1, groups)
    even = lax.rem(group, 2) == 0
    odd = lax.rem(group, 2) == 1
    lower = me < half
    upper = me >= half
    has_before, has_after = group > 0, group < groups - 1
    has_far = has_before & has_after
    chip_at = lax.rem((group - lax.rem(group + 1, 2) * 2 + groups) // 2, 4)
    first = (odd & (chip_at < 3)) | (even & (chip_at >= 3))
    second = (odd & (chip_at >= 3)) | (even & (chip_at < 3))
    near = lax.rem(group, 2) * before + (1 - lax.rem(group, 2)) * after
    far = lax.rem(group, 2) * after + (1 - lax.rem(group, 2)) * before

    def lanes(i):
        return pl.ds(pl.multiple_of(i * HEAD_DIM, HEAD_DIM), HEAD_DIM)

    def token_rows(part):
        return pl.ds(pl.multiple_of(part * rows, rows), rows)

    low_rows, high_rows = pl.ds(0, length // 2), pl.ds(length // 2, length // 2)

    def to(src, dst, send, recv, device):
        return pltpu.make_async_remote_copy(
            src_ref=src, dst_ref=dst, send_sem=send, recv_sem=recv,
            device_id=device, device_id_type=MESH,
        )

    def wait_bytes(ref, sem):
        pltpu.make_async_copy(ref, ref, sem).wait()

    def loads(i):
        pairs = ((k_hbm, k_own), (v_hbm, v_own), (q_hbm, q_own), (o_hbm, o_own))
        return [
            pltpu.make_async_copy(src.at[0, :, lanes(i)], dst.at[i], load_sem.at[at, i])
            for at, (src, dst) in enumerate(pairs)
        ]

    def local_g(i):
        return pltpu.make_async_copy(
            g_hbm.at[0, :, lanes(me * heads + i)], g_own.at[i, token_rows(me)], local_sem.at[i]
        )

    def key_copy(i):
        return to(k_hbm.at[0, :, lanes(i)], moved_a.at[i], a_sem.at[0, i], a_sem.at[1, i], (after, me))

    def value_copy(i):
        return to(v_hbm.at[0, :, lanes(i)], moved_b.at[i], b_sem.at[0, i], b_sem.at[1, i], (after, me))

    def query_copy(i):
        return to(q_hbm.at[0, :, lanes(i)], moved_a.at[i], a_sem.at[0, i], a_sem.at[1, i], (before, me))

    def g_high_copy(i):
        return to(
            g_own.at[i, high_rows], moved_b.at[i, high_rows], b_sem.at[0, i], b_sem.at[1, i], (before, me)
        )

    def g_low_copy(i):
        return to(
            g_own.at[i, low_rows], moved_b.at[i, low_rows], low_sem.at[0, i], low_sem.at[1, i], (before, me)
        )

    def delta_copy(i):
        return to(delta_own.at[i], delta_next.at[i], delta_sem.at[0, i], delta_sem.at[1, i], (before, me))

    def near_copy(which, i):
        return to(
            cross_out.at[which, i], cross_in.at[which, i],
            near_sem.at[0, which, i], near_sem.at[1, which, i], (near, me),
        )

    lse_copy = to(lse_hbm, lse_next, lse_sem.at[0], lse_sem.at[1], (before, me))

    barrier = pltpu.get_barrier_semaphore()

    @pl.loop(1, parts)
    def _(step):
        pl.semaphore_signal(
            barrier, inc=1, device_id=(group, lax.rem(me + step, parts)), device_id_type=MESH
        )

    pl.semaphore_signal(barrier, inc=1, device_id=(near, me), device_id_type=MESH)

    def greet_far(sem):
        @pl.loop(0, parts)
        def _(part):
            pl.semaphore_signal(sem, inc=1, device_id=(far, part), device_id_type=MESH)

    @pl.when(second & has_far)
    def _():
        pl.semaphore_wait(barrier, 2 * parts)
        greet_far(far_ready)

    @pl.when(first | jnp.logical_not(has_far))
    def _():
        pl.semaphore_wait(barrier, parts)

    @pl.when(first & has_far)
    def _():
        greet_far(barrier)

    @pl.loop(0, heads)
    def _(i):
        @pl.loop(1, parts)
        def _(step):
            peer = lax.rem(me + step, parts)
            to(
                g_hbm.at[0, :, lanes(peer * heads + i)], g_own.at[i, token_rows(me)],
                g_send, g_recv.at[i], (group, peer),
            ).start()

    @pl.when(first & has_far)
    def _():
        pl.semaphore_wait(far_ready, parts)

    @pl.loop(0, heads)
    def _(i):
        @pl.when(even & lower & has_before)
        def _():
            @pl.loop(0, half)
            def _(step):
                peer = half + lax.rem(me + step, half)
                to(
                    g_hbm.at[0, :, lanes(peer * heads + i)], moved_b.at[i, token_rows(me)],
                    direct_send, low_sem.at[1, i], (before, peer),
                ).start()

    @pl.loop(0, heads)
    def _(i):
        @pl.when(lower & has_after)
        def _():
            key_copy(i).start()
            value_copy(i).start()

        @pl.when(upper & has_before)
        def _():
            query_copy(i).start()

    small = ((lse_hbm, lse_own), (len_hbm, len_ref), (source_hbm, source_ref))
    small_loads = [pltpu.make_async_copy(src, dst, small_load.at[i]) for i, (src, dst) in enumerate(small)]
    for copy in small_loads:
        copy.start()
    @pl.loop(0, heads)
    def _(i):
        local_g(i).start()
        for copy in loads(i):
            copy.start()

    for copy in small_loads:
        copy.wait()
    own_len, before_len = len_ref[group], len_ref[before]
    linked_len = jnp.where(source_ref[group] == before, own_len, 0)
    after_len = jnp.where(source_ref[after] == group, len_ref[after], 0)
    query_at = lax.broadcasted_iota(jnp.int32, (1, length), 1)
    key_at = lax.broadcasted_iota(jnp.int32, (length, HEAD_DIM), 0)
    zero = jnp.zeros((), jnp.bfloat16)

    def own_row(i, live):
        return jnp.where(query_at < live, lse_own[i] * LOG2E, DEAD)

    def live_keys(k, live):
        return jnp.where(key_at < live, k, zero)

    def half_rows(x, live):
        return jnp.where(key_at < live, x, 0.0).astype(jnp.bfloat16)

    def send_out(which, i):
        columns = lanes(me * heads + i)

        @pl.loop(1, parts)
        def _(step):
            peer = lax.rem(me + step, parts)
            to(
                stage.at[which, i, token_rows(peer)], outs[which].at[0, :, columns],
                out_send.at[which], out_recv.at[which], (group, peer),
            ).start()

        pltpu.make_async_copy(
            stage.at[which, i, token_rows(me)], outs[which].at[0, :, columns], out_local.at[which]
        ).start()

    def send_far(which, i):
        columns = lanes(lax.rem(me, half) * heads + i)

        @pl.loop(0, parts)
        def _(step):
            peer = lax.rem(me + step, parts)
            to(
                cross_out.at[which, i, token_rows(peer)], land_far.at[which, :, columns],
                far_send.at[which], far_recv.at[which], (far, peer),
            ).start()

    def wait_g(i):
        wait_bytes(g_own.at[i, pl.ds(0, (parts - 1) * rows)], g_recv.at[i])
        local_g(i).wait()

    def own_delta(i):
        product = g_own[i].astype(jnp.float32) * o_own[i].astype(jnp.float32)
        delta = jnp.sum(product.T, axis=0, keepdims=True)
        delta_own[i] = delta
        return delta

    def own_block(i, delta):
        k = live_keys(k_own[i], own_len)
        return block_grads(q_own[i], g_own[i], own_row(i, own_len), delta, k, k.T, v_own[i])

    @pl.when(lower)
    def _():
        def finish_keys(i):
            near_copy(0, i).wait_recv()
            stage[1, i] = (acc_k[i] + cross_in[0, i].astype(jnp.float32)).astype(jnp.bfloat16)
            send_out(1, i)
            near_copy(1, i).wait_recv()
            stage[2, i] = (acc_v[i] + cross_in[1, i].astype(jnp.float32)).astype(jnp.bfloat16)
            send_out(2, i)

        @pl.loop(0, heads)
        def _(i):
            wait_g(i)
            for copy in loads(i):
                copy.wait()
            grad_q, grad_k, grad_v = own_block(i, own_delta(i))
            acc_q[i] = grad_q
            grad_k = jnp.where(key_at < own_len, grad_k * SCALE, 0.0)
            grad_v = jnp.where(key_at < own_len, grad_v, 0.0)

            @pl.when(even)
            def _():
                acc_k[i] = grad_k
                acc_v[i] = grad_v

            @pl.when(odd)
            def _():
                stage[1, i] = grad_k.astype(jnp.bfloat16)
                stage[2, i] = grad_v.astype(jnp.bfloat16)

        @pl.loop(0, heads)
        def _(i):
            @pl.when(has_before)
            def _():
                key_copy(i).wait_recv()
                value_copy(i).wait_recv()
                k = live_keys(moved_a[i], before_len)
                grad_q, grad_k, grad_v = block_grads(
                    q_own[i], g_own[i], own_row(i, linked_len), delta_own[i], k, k.T, moved_b[i]
                )
                cross_out[0, i] = half_rows(grad_k * SCALE, before_len)
                cross_out[1, i] = half_rows(grad_v, before_len)

                @pl.when(odd)
                def _():
                    near_copy(0, i).start()
                    near_copy(1, i).start()

                @pl.when(even)
                def _():
                    send_far(0, i)
                    send_far(1, i)

                stage[0, i] = ((acc_q[i] + grad_q) * SCALE).astype(jnp.bfloat16)

            @pl.when(jnp.logical_not(has_before))
            def _():
                stage[0, i] = (acc_q[i] * SCALE).astype(jnp.bfloat16)

            send_out(0, i)

            @pl.when(odd)
            def _():
                send_out(1, i)
                send_out(2, i)

            @pl.when(even & (i > 0))
            def _():
                finish_keys(i - 1)

        @pl.when(even)
        def _():
            finish_keys(heads - 1)

        @pl.when(even & has_before)
        def _():
            wait_bytes(cross_out.at[0], far_send.at[0])
            wait_bytes(cross_out.at[1], far_send.at[1])
            wait_bytes(g_hbm.at[0, :, pl.ds(0, half * heads * HEAD_DIM)], direct_send)

        @pl.loop(0, heads)
        def _(i):
            @pl.when(has_after)
            def _():
                key_copy(i).wait_send()
                value_copy(i).wait_send()

            @pl.when(odd)
            def _():
                near_copy(0, i).wait_send()
                near_copy(1, i).wait_send()

    @pl.when(upper)
    def _():
        @pl.when(has_before)
        def _():
            lse_copy.start()

        def finish_query(i):
            near_copy(0, i).wait_recv()
            stage[0, i] = (acc_q[i] * SCALE + cross_in[0, i].astype(jnp.float32)).astype(jnp.bfloat16)
            send_out(0, i)

        @pl.loop(0, heads)
        def _(i):
            wait_g(i)
            @pl.when(has_before)
            def _():
                g_high_copy(i).start()

            @pl.when(odd)
            def _():
                g_low_copy(i).start()

            for copy in loads(i):
                copy.wait()
            delta = own_delta(i)

            @pl.when(has_before)
            def _():
                delta_copy(i).start()

            grad_q, grad_k, grad_v = own_block(i, delta)
            acc_k[i] = grad_k
            acc_v[i] = grad_v

            @pl.when(even)
            def _():
                stage[0, i] = (grad_q * SCALE).astype(jnp.bfloat16)

            @pl.when(odd)
            def _():
                acc_q[i] = grad_q

        @pl.when(has_after)
        def _():
            lse_copy.wait_recv()

        @pl.loop(0, heads)
        def _(i):
            @pl.when(has_after)
            def _():
                query_copy(i).wait_recv()
                g_high_copy(i).wait_recv()
                g_low_copy(i).wait_recv()
                delta_copy(i).wait_recv()
                lse_row = jnp.where(query_at < after_len, lse_next[i] * LOG2E, DEAD)
                k = live_keys(k_own[i], own_len)
                grad_q, grad_k, grad_v = block_grads(
                    moved_a[i], moved_b[i], lse_row, delta_next[i], k, k.T, v_own[i]
                )
                cross_out[0, i] = (grad_q * SCALE).astype(jnp.bfloat16)

                @pl.when(even)
                def _():
                    near_copy(0, i).start()

                @pl.when(odd)
                def _():
                    send_far(0, i)

                stage[1, i] = half_rows((acc_k[i] + grad_k) * SCALE, own_len)
                stage[2, i] = half_rows(acc_v[i] + grad_v, own_len)

            @pl.when(jnp.logical_not(has_after))
            def _():
                stage[1, i] = half_rows(acc_k[i] * SCALE, own_len)
                stage[2, i] = half_rows(acc_v[i], own_len)

            send_out(1, i)
            send_out(2, i)

            @pl.when(even)
            def _():
                send_out(0, i)

            @pl.when(odd & (i > 0))
            def _():
                finish_query(i - 1)

        @pl.when(odd)
        def _():
            finish_query(heads - 1)

        @pl.when(odd & has_after)
        def _():
            wait_bytes(cross_out.at[0], far_send.at[0])

        @pl.when(has_before)
        def _():
            lse_copy.wait_send()

        @pl.loop(0, heads)
        def _(i):
            @pl.when(has_before)
            def _():
                query_copy(i).wait_send()
                g_high_copy(i).wait_send()
                delta_copy(i).wait_send()

            @pl.when(odd)
            def _():
                g_low_copy(i).wait_send()

            @pl.when(even)
            def _():
                near_copy(0, i).wait_send()

    wait_bytes(g_hbm.at[0, :, pl.ds(0, (parts - 1) * heads * HEAD_DIM)], g_send)
    for which in range(3):
        theirs = outs[which].at[0, :, pl.ds(0, (parts - 1) * heads * HEAD_DIM)]
        wait_bytes(theirs, out_recv.at[which])
        wait_bytes(theirs, out_send.at[which])
        wait_bytes(outs[which].at[0, :, pl.ds(0, heads * HEAD_DIM)], out_local.at[which])

    low = pl.ds(0, half * heads * HEAD_DIM)
    high = pl.ds(half * heads * HEAD_DIM, half * heads * HEAD_DIM)

    def add_far(out, columns, far_at):
        total = out[0, :, columns].astype(jnp.float32) + land_far[far_at].astype(jnp.float32)
        out[0, :, columns] = total.astype(jnp.bfloat16)

    @pl.when(has_far)
    def _():
        wait_bytes(land_far.at[0], far_recv.at[0])

    @pl.when(even & has_far)
    def _():
        add_far(out_q, high, 0)

    @pl.when(odd & has_far)
    def _():
        wait_bytes(land_far.at[1], far_recv.at[1])
        add_far(out_k, low, 0)
        add_far(out_v, low, 1)


def write_kernel(in_q, in_k, in_v, out_q, out_k, out_v, sems):
    pairs = ((in_q, out_q), (in_k, out_k), (in_v, out_v))
    copies = [pltpu.make_async_copy(src, dst, sems.at[i]) for i, (src, dst) in enumerate(pairs)]
    for copy in copies:
        copy.start()
    for copy in copies:
        copy.wait()


def on_device(query, key, value, output, grad_out, log_sum, group_length, cache_source):
    _, length, features = query.shape
    heads = features // HEAD_DIM
    per_head = (heads, length, HEAD_DIM)
    half = pltpu.VMEM(per_head, jnp.bfloat16)
    wide = pltpu.VMEM(per_head, jnp.float32)
    row = pltpu.VMEM((heads, 1, length), jnp.float32)
    dma = pltpu.SemaphoreType.DMA
    anywhere = pl.BlockSpec(memory_space=pl.ANY)
    vmem = pl.BlockSpec(memory_space=pltpu.VMEM)
    out = jax.ShapeDtypeStruct(grad_out.shape, jnp.bfloat16)
    flops = 10 * 2 * heads * length * length * HEAD_DIM
    rows_first = log_sum.transpose(1, 0, 2)
    inputs = (group_length, cache_source, query, key, value, output, grad_out, rows_first)
    landed = pl.pallas_call(
        kernel,
        out_shape=(out, out, out),
        in_specs=[anywhere] * 8,
        out_specs=(vmem, vmem, vmem),
        scratch_shapes=[
            pltpu.SMEM(group_length.shape, jnp.int32), pltpu.SMEM(cache_source.shape, jnp.int32),
            half, half, half, half, half, half, half,
            row, row, row, row,
            wide, wide, wide,
            pltpu.VMEM((3,) + per_head, jnp.bfloat16), pltpu.VMEM((2,) + per_head, jnp.bfloat16),
            pltpu.VMEM((2,) + per_head, jnp.bfloat16),
            pltpu.VMEM((2, grad_out.shape[1], grad_out.shape[2] // 2), jnp.bfloat16),
            dma((4, heads)), dma((heads,)), dma, dma((heads,)), dma((3,)), dma((2,)), dma((2, heads)),
            dma((2, heads)), dma((2, heads)), dma, dma((2, heads)),
            dma((2, 2, heads)), dma((2,)), dma((2,)), dma((3,)), dma((3,)), dma((3,)),
            pltpu.SemaphoreType.REGULAR,
        ],
        compiler_params=pltpu.CompilerParams(
            collective_id=0, has_side_effects=True, vmem_limit_bytes=40 * 1024 * 1024
        ),
        cost_estimate=pl.CostEstimate(
            flops=flops, bytes_accessed=8 * length * features * 2, transcendentals=2 * heads * length * length
        ),
        name="attention_backward",
    )(*[pltpu.with_memory_space_constraint(x, pltpu.HBM) for x in inputs])
    return pl.pallas_call(
        write_kernel,
        out_shape=(out, out, out),
        in_specs=[vmem] * 3,
        out_specs=(anywhere, anywhere, anywhere),
        scratch_shapes=[dma((3,))],
        cost_estimate=pl.CostEstimate(flops=0, bytes_accessed=6 * out.size * 2, transcendentals=0),
        compiler_params=pltpu.CompilerParams(vmem_limit_bytes=16 * 1024 * 1024),
        name="write_out",
    )(*landed)


def solution(mesh):
    by_head, by_token = P("group", None, "head"), P("group", "head", None)
    return jax.shard_map(
        on_device,
        mesh=mesh,
        in_specs=(by_head, by_head, by_head, by_head, by_token, by_token, P(), P()),
        out_specs=(by_token, by_token, by_token),
        check_vma=False,
    )
```
